256 devices in a mesh: dp: 16 (over z, y_lo), row: 4 (over x), col: 4 (over y_hi, core).
Axes of the slice: x: 4, y: 4 (y_hi: 2, y_lo: 2; y = y_hi * 2 + y_lo), z: 8, core: 2. Of those that a mesh axis runs over, the one named last changes fastest.
Arguments:
- inputs: bfloat16 [16, 96, 7680], P('dp', 'row', 'col'), may hold values from -6 to 6
- levels: bfloat16 [7680, 32768], P('row', ('dp', 'col')), may hold values from -4 to 4
- block_scales: float32 [60, 256], P('row', ('dp', 'col')), may hold values from 0.005705443 to 0.045643546
- grad_hidden: bfloat16 [16, 96, 32768], P(None, 'row', ('dp', 'col')), may hold values from -6 to 6
Outputs:
- hidden: bfloat16 [16, 96, 32768], P(None, 'row', ('dp', 'col'))
- grad_inputs: bfloat16 [16, 96, 7680], P('dp', 'row', 'col')
- grad_weight: bfloat16 [7680, 32768], P('row', ('dp', 'col'))
The draws below stay inside these ranges and needn't reach their ends.
All inputs are finite; a program needn't handle non-finite values.
Results may differ from the reference program's by a relative error of at most 0.02.
Values may be sent and summed in bfloat16 or wider, within the bound.
A program may use at most 128 MiB of HBM per device.

```python
import math
import jax
import jax.numpy as jnp
from jax import lax

D = 7680
FF = 32768
BLOCK = 128
TOK_REP = 96
REPLICAS = 16
N_ROW = 4


def with_spikes(array, key, source, target, parts, factor):
    def block_of(position):
        return (jnp.arange(array.shape[position]) // (array.shape[position] // parts)).reshape((-1,) + (1,) * (array.ndim - 1 - position))

    one_side = jax.random.permutation(key, parts)[block_of(target)]
    other_side = (block_of(target) + parts // 2) % parts
    return jnp.where((block_of(source) == one_side) | (block_of(source) == other_side), factor * array, array)


def block_scale(key, dims, cuts, low, high):
    loudness, own = 1.0, jax.random.fold_in(key, 6)
    for axis_at, blocks in cuts:
        heights = jnp.exp(jax.random.uniform(jax.random.fold_in(own, axis_at), (blocks,), jnp.float32, low / len(cuts), high / len(cuts)))
        loudness = loudness * jnp.repeat(heights, dims[axis_at] // blocks).reshape([-1 if axis == axis_at else 1 for axis in range(len(dims))])
    return loudness


def noise(own_key, extent, spread, limit, shards=(), kind=jnp.bfloat16):
    result = spread * jax.random.normal(own_key, extent, jnp.float32)
    if shards:
        result = result * block_scale(own_key, extent, shards, -0.22, 0.18)
    return jnp.clip(result, -limit, limit).astype(kind)


def bell_draw_with(rng, shape, width, bound, pieces, heavy, dtype=jnp.bfloat16):
    drawn = width * jax.random.normal(rng, shape, jnp.float32)
    if pieces:
        drawn = drawn * block_scale(rng, shape, pieces, -0.22, 0.18)
    return jnp.clip(with_spikes(drawn, jax.random.fold_in(rng, 3), *heavy), -bound, bound).astype(dtype)


def setup_inputs(seed: int = 0) -> dict:
    arg_keys = jax.random.split(jax.random.key(seed), 5)
    inputs = noise(arg_keys[0], (REPLICAS, TOK_REP, D), 1.0, 6.0, ((0, 16), (1, 4), (2, 4)))
    levels = noise(arg_keys[1], (D, FF), 1.0, 4.0, ((0, 4), (1, 64)))
    block_scales = jnp.clip(jnp.exp(math.log(0.045643546) - 2.0794415 * jax.random.uniform(arg_keys[2], (D // BLOCK, FF // BLOCK), jnp.float32) ** block_scale(arg_keys[2], (D // BLOCK, FF // BLOCK), ((0, 4), (1, 64)), -0.2, 0.2)), 0.005705443, 0.045643546)
    grad_hidden = bell_draw_with(arg_keys[3], (REPLICAS, TOK_REP, FF), 1.0, 6.0, ((1, 4), (2, 64)), (2, 0, 16, 2.0))
    return dict(inputs=inputs, levels=levels, block_scales=block_scales, grad_hidden=grad_hidden)


inv_root_two = 0.7071067811865476
inv_root_two_pi = 0.3989422804014327


def gelu_pair(pre):
    normal_cdf = 0.5 * (1.0 + jax.scipy.special.erf(pre * inv_root_two))
    density = jnp.exp(-0.5 * pre * pre) * inv_root_two_pi
    return pre * normal_cdf, normal_cdf + pre * density


def reference(inputs, levels, block_scales, grad_hidden):
    nrow_blocks, ncol_blocks = block_scales.shape
    scaled = levels.reshape(nrow_blocks, BLOCK, ncol_blocks, BLOCK) * block_scales[:, None, :, None]
    weight = scaled.reshape(D, FF).astype(jnp.bfloat16)
    tok_rows = inputs.reshape(-1, D)
    pre = jnp.dot(tok_rows, weight, preferred_element_type=jnp.float32)
    activated, slope = gelu_pair(pre)
    hidden = activated.astype(jnp.bfloat16).reshape(grad_hidden.shape)
    grad_pre = (grad_hidden.reshape(-1, FF).astype(jnp.float32) * slope).astype(jnp.bfloat16)
    grad_inputs = jnp.dot(grad_pre, weight.T, preferred_element_type=jnp.float32).astype(jnp.bfloat16).reshape(inputs.shape)
    grad_three = grad_pre.reshape(grad_hidden.shape)
    block_tokens = TOK_REP // N_ROW
    summed = jnp.zeros((D, FF), jnp.float32)
    for which in range(N_ROW):
        part_inputs = inputs[:, which * block_tokens:(which + 1) * block_tokens, :].reshape(-1, D)
        part_grads = grad_three[:, which * block_tokens:(which + 1) * block_tokens, :].reshape(-1, FF)
        term = jnp.dot(part_inputs.T, part_grads, preferred_element_type=jnp.float32).astype(jnp.bfloat16)
        term = lax.optimization_barrier(term)
        summed = summed + term.astype(jnp.float32)
    return hidden, grad_inputs, summed.astype(jnp.bfloat16)
```

```python
import jax
import jax.numpy as jnp
from jax import lax
from jax.sharding import PartitionSpec as P

inv_root_two = 0.7071067811865476
inv_root_two_pi = 0.3989422804014327


def gelu_pair(pre):
    normal_cdf = 0.5 * (1.0 + jax.scipy.special.erf(pre * inv_root_two))
    density = jnp.exp(-0.5 * pre * pre) * inv_root_two_pi
    return (pre * normal_cdf, normal_cdf + pre * density)


def swap_row_col(x, n):
    return lax.ppermute(x, ("row", "col"), [(r * n + c, c * n + r) for r in range(n) for c in range(n)])


def shards(inputs, levels, block_scales, grad_hidden):
    nrow_blocks, ncol_blocks = block_scales.shape
    side = levels.shape[0] // nrow_blocks
    scaled = levels.reshape(nrow_blocks, side, ncol_blocks, side) * block_scales[:, None, :, None]
    weight = scaled.reshape(levels.shape).astype(jnp.bfloat16)
    n = lax.axis_size("row")
    block_tokens, feats = inputs.shape[1:]
    replicas = grad_hidden.shape[0]
    mine = swap_row_col(inputs[0], n)
    tok_rows = lax.all_gather(mine, ("dp", "col"), axis=0, tiled=False).reshape(replicas, n, block_tokens, feats)
    tok_rows = tok_rows.transpose(1, 0, 2, 3).reshape(n * replicas * block_tokens, feats)
    part = jnp.dot(tok_rows, weight, preferred_element_type=jnp.float32).astype(jnp.bfloat16)
    pre = lax.psum_scatter(part, "row", scatter_dimension=0, tiled=True).astype(jnp.float32)
    activated, slope = gelu_pair(pre)
    hidden = activated.astype(jnp.bfloat16).reshape(grad_hidden.shape)
    grad_pre = (grad_hidden.reshape(pre.shape).astype(jnp.float32) * slope).astype(jnp.bfloat16)
    all_grad = lax.all_gather(grad_pre, "row", axis=0, tiled=True)
    product = lax.dot_general(
        all_grad, weight, (((1,), (1,)), ((), ())), preferred_element_type=jnp.float32
    ).astype(jnp.bfloat16)
    terms = product.reshape(n, replicas, block_tokens, feats).transpose(1, 0, 2, 3).reshape(-1, feats)
    own = lax.psum_scatter(terms, ("dp", "col"), scatter_dimension=0, tiled=True)
    grad_inputs = swap_row_col(own.astype(jnp.bfloat16), n)[None]
    grad_weight = lax.dot_general(
        tok_rows, all_grad, (((0,), (0,)), ((), ())), preferred_element_type=jnp.float32
    ).astype(jnp.bfloat16)
    return (hidden, grad_inputs, grad_weight)


def solution(mesh):
    placed = (
        P("dp", "row", "col"),
        P("row", ("dp", "col")),
        P("row", ("dp", "col")),
        P(None, "row", ("dp", "col")),
    )
    return jax.shard_map(
        shards,
        mesh=mesh,
        in_specs=placed,
        out_specs=(P(None, "row", ("dp", "col")), P("dp", "row", "col"), P("row", ("dp", "col"))),
        check_vma=False,
    )
```

```python
import functools

import jax
import jax.numpy as jnp
from jax import lax
from jax.experimental import pallas as pl
from jax.experimental.pallas import tpu as pltpu
from jax.sharding import PartitionSpec as P

inv_root_two = 0.7071067811865476
inv_root_two_pi = 0.3989422804014327
bf16, f32 = jnp.bfloat16, jnp.float32

NZ, NY, NX = 8, 4, 4
ROWS = 48
U = 16
D4 = 1920
H = 512
BW = 1024
BO = 896
GROUPS = ((0, 3), (3, 5), (5, 8))
N_SEND, N_RECV = 144, 144


def pos_f(k):
    return 0 if k == 0 else 2 * k - 1


def pos_b(k):
    return 2 * k


def sib_pos(p):
    if p == 0 or p == 7:
        return p
    return p + 1 if p % 2 else p - 1


def gelu_pair(pre):
    normal_cdf = 0.5 * (1.0 + lax.erf(pre * inv_root_two))
    density = jnp.exp(-0.5 * pre * pre) * inv_root_two_pi
    return (pre * normal_cdf, normal_cdf + pre * density)


def kernel(inp, lev, scl, gh, hid, gin, gw,
           W, S0, R0, X, PS, PR, GP, GI, CA, CB,
           A1s, Ass, A2s, A1r, Asr, A2r, YA,
           ZLs, ZLr, ZSs, ZSr, BLs, BLr, BSs, BSr, YB,
           Y1s, Yss, Y2s, Y1r, Ysr, Y2r, FA, FB, OA, OB,
           ssem, rsem):
    dp, x, col = lax.axis_index("dp"), lax.axis_index("row"), lax.axis_index("col")
    z, ylo, yhi, core = dp // 2, dp % 2, col // 2, col % 2
    y = 2 * yhi + ylo
    s = 1 - 2 * core

    def dev(zz, yy, xx, cc):
        return {"dp": zz * 2 + yy % 2, "row": xx, "col": (yy // 2) * 2 + cc}

    sources = [dev(z, 2 * (x // 2) + j, y, x % 2) for j in range(2)]
    targets = [dev(z, x, 2 * yhi + core, c) for c in range(2)]
    loops = (x == y) & (core == x % 2)
    z_f, z_b = dev((z + s + NZ) % NZ, y, x, core), dev((z - s + NZ) % NZ, y, x, core)
    y_f, y_b = dev(z, (y + s + NY) % NY, x, core), dev(z, (y - s + NY) % NY, x, core)
    sib = dev(z, y, x, 1 - core)
    yf1, yb1, yf2 = (y - s + NY) % NY, (y + s + NY) % NY, (y + 2) % NY
    x_dev = [None] + [dev(z, y, (x + d) % NX, core) for d in range(1, NX)]

    sends, keys, sent = [], {}, [0]

    def rid(key):
        if key not in keys:
            keys[key] = len(keys)
        return rsem.at[keys[key]]

    def copy(src, dst, key, to):
        i = sent[0]
        sent[0] += 1
        return pltpu.make_async_remote_copy(src, dst, ssem.at[i], rid(key), device_id=to)

    def send(src, dst, key, to):
        c = copy(src, dst, key, to)
        c.start()
        sends.append(c)

    def arrived(dst, key):
        pltpu.make_async_remote_copy(dst, dst, ssem.at[0], rid(key), device_id=sib).wait_recv()

    bar = pltpu.get_barrier_semaphore()
    partners = sources + targets + x_dev[1:] + [z_f, z_b, y_f, y_b, sib]
    for d in partners:
        pl.semaphore_signal(bar, 1, device_id=d)
    S0[...] = jnp.concatenate([inp[...].astype(f32), jnp.zeros((8, D4), f32)], 0).astype(bf16)
    pl.semaphore_wait(bar, len(partners))

    slot = ylo
    swaps = []
    for c in range(2):
        i = sent[0]
        sent[0] += 1
        swaps.append(pltpu.make_async_remote_copy(S0, R0.at[slot], ssem.at[i], rsem.at[slot], device_id=targets[c]))
    for j in range(2):
        rid(("swap", j))
    for c in range(2):
        mine = loops & (core == c)

        @pl.when(jnp.logical_not(mine))
        def _():
            swaps[c].start()

        @pl.when(mine)
        def _():
            R0[slot] = S0[...]

    @pl.loop(0, D4 // 128)
    def _(a):
        r = pl.ds(pl.multiple_of(a * 128, 128), 128)
        for b in range(H // 128):
            cs = pl.ds(b * 128, 128)
            W[r, cs] = (lev[r, cs].astype(f32) * scl[a, b]).astype(bf16)

    for j in range(2):

        @pl.when(jnp.logical_not(loops & (j == x % 2)))
        def _():
            arrived(R0.at[j], ("swap", j))

    X[y, 0] = jnp.concatenate([R0[0].astype(f32)[:24], R0[1].astype(f32)[:24]], 0).astype(bf16)

    r_mine = pl.ds(pl.multiple_of(core * U, U), U)
    r_other = pl.ds(pl.multiple_of((1 - core) * U, U), U)
    r_b = pl.ds(2 * U, U)
    c_mine = pl.ds(pl.multiple_of(core * BO, 128), BW)
    c_other = pl.ds(pl.multiple_of((1 - core) * BO, 128), BW)
    c_give = pl.ds(pl.multiple_of(core * BW, 128), BO)
    c_take = pl.ds(pl.multiple_of((1 - core) * BW, 128), BO)

    def a_unit(yq, p):
        return X.at[yq, p, r_mine]

    def b_unit(yq, p):
        return X.at[yq, p, r_b, c_mine]

    def b_group(p):
        return X.at[:, p, r_b, c_mine]

    def at_dist(k):
        return [0] if k == 0 else [pos_f(k)] + ([pos_b(k)] if k < 4 else [])

    def y_start(p):
        send(a_unit(y, p), a_unit(y, p), ("Ay", p, 1), y_f)
        send(a_unit(y, p), a_unit(y, p), ("Ay", p, -1), y_b)

    def y_hop1(p):
        arrived(a_unit(yf1, p), ("Ay", p, 1))
        send(a_unit(yf1, p), a_unit(yf1, p), ("Ay", p, 2), y_f)
        if p == 0:
            send(a_unit(yf1, 0), a_unit(yf1, 0), ("As0", -1), sib)
        arrived(a_unit(yb1, p), ("Ay", p, -1))
        if p == 0:
            send(a_unit(yb1, 0), a_unit(yb1, 0), ("As0", 1), sib)

    def y_hop2(p):
        arrived(a_unit(yf2, p), ("Ay", p, 2))
        if p == 0:
            send(a_unit(yf2, 0), a_unit(yf2, 0), ("As0", 2), sib)
        else:
            send(X.at[:, p, r_mine], X.at[:, sib_pos(p), r_mine], ("As", sib_pos(p)), sib)

    def bz_send(k):
        if k < 4:
            send(b_group(pos_f(k)), b_group(pos_f(k + 1)), ("Bz", pos_f(k + 1)), z_f)
        if k < 3:
            send(b_group(pos_b(k)), b_group(pos_b(k + 1)), ("Bz", pos_b(k + 1)), z_b)

    def bz_hop(k):
        for p in at_dist(k):
            arrived(b_group(p), ("Bz", p))
        bz_send(k)
        for p in at_dist(k):
            send(X.at[:, p, r_b, c_give], X.at[:, sib_pos(p), r_b, c_give], ("Bs", sib_pos(p)), sib)

    def sib_wait(k):
        for p in at_dist(k):
            if p == 0:
                for q, yq in ((1, yf1), (-1, yb1), (2, yf2)):
                    arrived(X.at[yq, 0, r_other], ("As0", q))
                    arrived(X.at[yq, 0, r_b, c_take], ("Bs0", q))
            else:
                arrived(X.at[:, p, r_other], ("As", p))
                arrived(X.at[:, p, r_b, c_take], ("Bs", p))

    def az_send(k):
        if k < 4:
            send(a_unit(y, pos_f(k)), a_unit(y, pos_f(k + 1)), ("Az", pos_f(k + 1)), z_f)
        if k < 3:
            send(a_unit(y, pos_b(k)), a_unit(y, pos_b(k + 1)), ("Az", pos_b(k + 1)), z_b)

    def tick(k):
        if k == 0:
            az_send(0)
            y_start(0)
            send(b_unit(y, 0), b_unit(y, 0), ("By", 1), y_f)
            send(b_unit(y, 0), b_unit(y, 0), ("By", -1), y_b)
            return
        if k <= 4:
            for p in at_dist(k):
                arrived(a_unit(y, p), ("Az", p))
            az_send(k)
            for p in at_dist(k):
                y_start(p)
        if k == 1:
            arrived(b_unit(yf1, 0), ("By", 1))
            send(b_unit(yf1, 0), b_unit(yf1, 0), ("By", 2), y_f)
            arrived(b_unit(yb1, 0), ("By", -1))
            send(X.at[yf1, 0, r_b, c_give], X.at[yf1, 0, r_b, c_give], ("Bs0", -1), sib)
            send(X.at[yb1, 0, r_b, c_give], X.at[yb1, 0, r_b, c_give], ("Bs0", 1), sib)
        if k == 2:
            arrived(b_unit(yf2, 0), ("By", 2))
            bz_send(0)
            send(X.at[yf2, 0, r_b, c_give], X.at[yf2, 0, r_b, c_give], ("Bs0", 2), sib)
        if k - 1 <= 4:
            for p in at_dist(k - 1):
                y_hop1(p)
        if 3 <= k <= 6:
            bz_hop(k - 2)
        if k >= 2:
            for p in at_dist(k - 2):
                y_hop2(p)

    def partial_pre(g):
        p0, p1 = GROUPS[g]
        m = (p1 - p0) * ROWS
        for h in range(0, H, 256):
            rows = X[:, p0:p1].reshape(NY * m, D4)
            part = jnp.dot(rows, W[:, h:h + 256], preferred_element_type=f32)
            PS[:, p0:p1, :, h:h + 256] = part.astype(bf16).reshape(NY, p1 - p0, ROWS, 256)
        for d in range(1, NX):
            t = (x + d) % NX
            send(PS.at[t, p0:p1], PR.at[d - 1, p0:p1], ("pre", g, d), x_dev[d])

    def activate(g):
        p0, p1 = GROUPS[g]
        for d in range(1, NX):
            arrived(PR.at[d - 1, p0:p1], ("pre", g, d))

        @pl.loop(p0, p1)
        def _(p):
            k = (p + 1) // 2
            zz = (z + (1 - 2 * (p % 2)) * k * s + NZ) % NZ
            pre = PS[x, p].astype(f32)
            for d in range(NX - 1):
                pre += PR[d, p].astype(f32)
            activated, slope = gelu_pair(pre)
            hid[zz] = activated.astype(bf16)
            GP[x, p] = (gh[zz].astype(f32) * slope).astype(bf16)

        for d in range(1, NX):
            send(GP.at[x, p0:p1], GP.at[x, p0:p1], ("gp", g, d), x_dev[d])

    def grad_wait(g):
        p0, p1 = GROUPS[g]
        for d in range(1, NX):
            arrived(GP.at[(x - d + NX) % NX, p0:p1], ("gp", g, d))

    def input_terms(g):
        p0, p1 = GROUPS[g]
        m = (p1 - p0) * ROWS
        grad_wait(g)

        @pl.loop(0, D4 // 384)
        def _(n):
            cs = pl.ds(pl.multiple_of(n * 384, 128), 384)
            rows = GP[:, p0:p1].reshape(NY * m, H)
            part = lax.dot_general(rows, W[cs, :], (((1,), (1,)), ((), ())), preferred_element_type=f32)
            GI[:, p0:p1, :, cs] = part.astype(bf16).reshape(NY, p1 - p0, ROWS, 384)

        for p in reversed(range(p0, p1)):
            q = sib_pos(p)
            send(GI.at[:, p, r_b, c_other], CB.at[:, q], ("CB", q), sib)
            send(GI.at[:, p, r_other], CA.at[:, q], ("CA", q), sib)

    def a_term(yq, p):
        return GI[yq, p, r_mine].astype(f32) + CA[yq, p].astype(f32)

    def ay_begin(g):
        p0, p1 = GROUPS[g]
        for p in range(p0, p1):
            arrived(CA.at[:, p], ("CA", p))

        @pl.loop(p0, p1)
        def _(p):
            A1s[p] = a_term(yf2, p).astype(bf16)
            Ass[p] = a_term(yb1, p).astype(bf16)

        send(A1s.at[p0:p1], A1r.at[p0:p1], ("A1", g), y_b)
        send(Ass.at[p0:p1], Asr.at[p0:p1], ("As_", g), y_f)

    def ay_middle(g):
        p0, p1 = GROUPS[g]
        arrived(A1r.at[p0:p1], ("A1", g))

        @pl.loop(p0, p1)
        def _(p):
            A2s[p] = (a_term(yf1, p) + A1r[p].astype(f32)).astype(bf16)

        send(A2s.at[p0:p1], A2r.at[p0:p1], ("A2", g), y_b)

    def ay_end(g):
        p0, p1 = GROUPS[g]
        arrived(Asr.at[p0:p1], ("As_", g))
        arrived(A2r.at[p0:p1], ("A2", g))

        @pl.loop(p0, p1)
        def _(p):
            YA[p] = a_term(y, p) + Asr[p].astype(f32) + A2r[p].astype(f32)

    def b_terms(p):
        return GI[:, p, r_b, c_mine].astype(f32) + CB[:, p].astype(f32)

    def z_chain(j, term, ls, lr, ss, sr, name):
        if j == 0:
            ls[0] = term(pos_f(4)).astype(bf16)
            ss[0] = term(pos_b(3)).astype(bf16)
        else:
            arrived(lr.at[j - 1], (name, "L", j))
            if j < 4:
                ls[j] = (term(pos_f(4 - j)) + lr[j - 1].astype(f32)).astype(bf16)
            if j < 4:
                arrived(sr.at[j - 1], (name, "S", j))
            if j < 3:
                ss[j] = (term(pos_b(3 - j)) + sr[j - 1].astype(f32)).astype(bf16)
        if j < 4:
            send(ls.at[j], lr.at[j], (name, "L", j + 1), z_b)
        if j < 3:
            send(ss.at[j], sr.at[j], (name, "S", j + 1), z_f)
        if j == 4:
            return term(0) + lr[3].astype(f32) + sr[2].astype(f32)

    def weight_grad(n0, n1):
        @pl.loop(n0, n1)
        def _(n):
            cs = pl.ds(pl.multiple_of(n * 128, 128), 128)
            rows = X[:, :, :, cs].reshape(NY * NZ * ROWS, 128)
            part = lax.dot_general(
                rows, GP[...].reshape(NY * NZ * ROWS, H), (((0,), (0,)), ((), ())), preferred_element_type=f32
            )
            gw[cs, :] = part.astype(bf16)

    for k in range(4):
        tick(k)
    sib_wait(0)
    sib_wait(1)
    partial_pre(0)
    tick(4)
    sib_wait(2)
    partial_pre(1)
    tick(5)
    activate(0)
    tick(6)
    sib_wait(3)
    sib_wait(4)
    partial_pre(2)
    activate(1)
    input_terms(0)
    input_terms(1)
    ay_begin(0)
    activate(2)
    ay_middle(0)
    ay_begin(1)
    ay_end(0)
    input_terms(2)
    ay_middle(1)
    for p in range(NZ):
        arrived(CB.at[:, p], ("CB", p))
    z_chain(0, b_terms, BLs, BLr, BSs, BSr, "B")
    ay_begin(2)
    ay_end(1)
    weight_grad(0, 4)
    z_chain(1, b_terms, BLs, BLr, BSs, BSr, "B")
    ay_middle(2)
    weight_grad(4, 8)
    z_chain(2, b_terms, BLs, BLr, BSs, BSr, "B")
    ay_end(2)
    a_final = functools.partial(z_chain, term=lambda p: YA[p], ls=ZLs, lr=ZLr, ss=ZSs, sr=ZSr, name="A")
    a_final(0)
    weight_grad(8, 11)
    z_chain(3, b_terms, BLs, BLr, BSs, BSr, "B")
    a_final(1)
    weight_grad(11, 15)
    YB[...] = z_chain(4, b_terms, BLs, BLr, BSs, BSr, "B")
    Y1s[...] = YB[yf2].astype(bf16)
    Yss[...] = YB[yb1].astype(bf16)
    send(Y1s, Y1r, ("Y1",), y_b)
    send(Yss, Ysr, ("Ys",), y_f)
    a_final(2)
    arrived(Y1r, ("Y1",))
    Y2s[...] = (YB[yf1] + Y1r[...].astype(f32)).astype(bf16)
    send(Y2s, Y2r, ("Y2",), y_b)
    a_final(3)
    arrived(Ysr, ("Ys",))
    arrived(Y2r, ("Y2",))
    FB[...] = (YB[y] + Ysr[...].astype(f32) + Y2r[...].astype(f32)).astype(bf16)
    FA[...] = a_final(4).astype(bf16)

    backs = []
    for j in range(2):
        for src, dst, name in ((FA, OA, "OA"), (FB, OB, "OB")):
            i = sent[0]
            sent[0] += 1
            first = rid((name, 0))
            second = rid((name, 1))
            base = keys[(name, 0)]
            backs.append((j, pltpu.make_async_remote_copy(src, dst.at[core], ssem.at[i], rsem.at[base + core], device_id=sources[j])))
    for j, c in backs:

        @pl.when(jnp.logical_not(loops & (j == x % 2)))
        def _():
            c.start()

    @pl.when(loops)
    def _():
        OA[core] = FA[...]
        OB[core] = FB[...]

    for c in range(2):

        @pl.when(jnp.logical_not(loops & (core == c)))
        def _():
            arrived(OA.at[c], ("OA", c))
            arrived(OB.at[c], ("OB", c))

    a0, a1 = OA[0].astype(f32), OA[1].astype(f32)

    @pl.when(ylo == 0)
    def _():
        gin[...] = jnp.concatenate([a0, a1[:8]], 0).astype(bf16)

    @pl.when(ylo == 1)
    def _():
        last = jnp.concatenate([OB[0].astype(f32), OB[1].astype(f32)[:, 2 * BW - D4:]], 1)
        gin[...] = jnp.concatenate([a1[8:], last], 0).astype(bf16)

    for c in range(2):

        @pl.when(jnp.logical_not(loops & (core == c)))
        def _():
            swaps[c].wait_send()

    for j, c in backs:

        @pl.when(jnp.logical_not(loops & (j == x % 2)))
        def _():
            c.wait_send()

    for c in sends:
        c.wait_send()
    assert sent[0] <= N_SEND and len(keys) <= N_RECV, (sent, len(keys))


def shards(inputs, levels, block_scales, grad_hidden):
    vm = lambda *shape: pltpu.VMEM(shape, bf16)
    vf = lambda *shape: pltpu.VMEM(shape, f32)
    vmem, smem = pl.BlockSpec(memory_space=pltpu.VMEM), pl.BlockSpec(memory_space=pltpu.SMEM)
    a_buf = vm(NZ, U, D4)
    y_buf = vm(U, BW)
    hidden, grad_inputs, grad_weight = pl.pallas_call(
        kernel,
        out_shape=(
            jax.ShapeDtypeStruct((NZ, ROWS, H), bf16),
            jax.ShapeDtypeStruct((24, D4), bf16),
            jax.ShapeDtypeStruct((D4, H), bf16),
        ),
        in_specs=[vmem, vmem, smem, vmem],
        out_specs=(vmem, vmem, vmem),
        scratch_shapes=[
            vm(D4, H),
            vm(32, D4), vm(2, 32, D4),
            vm(NY, NZ, ROWS, D4),
            vm(NY, NZ, ROWS, H), vm(NX - 1, NZ, ROWS, H), vm(NY, NZ, ROWS, H),
            vm(NY, NZ, ROWS, D4), vm(NY, NZ, U, D4), vm(NY, NZ, U, BW),
            a_buf, a_buf, a_buf, a_buf, a_buf, a_buf, vf(NZ, U, D4),
            vm(4, U, D4), vm(4, U, D4), vm(3, U, D4), vm(3, U, D4),
            vm(4, NY, U, BW), vm(4, NY, U, BW), vm(3, NY, U, BW), vm(3, NY, U, BW), vf(NY, U, BW),
            y_buf, y_buf, y_buf, y_buf, y_buf, y_buf,
            vm(U, D4), y_buf, vm(2, U, D4), vm(2, U, BW),
            pltpu.SemaphoreType.DMA((N_SEND,)),
            pltpu.SemaphoreType.DMA((N_RECV,)),
        ],
        compiler_params=pltpu.CompilerParams(
            collective_id=0, has_side_effects=True, vmem_limit_bytes=60 * 2**20
        ),
        name="grid_layer",
    )(inputs[0], levels, block_scales, grad_hidden.reshape(NZ, ROWS, H))
    return (hidden.reshape(grad_hidden.shape), grad_inputs[None], grad_weight)


def solution(mesh):
    placed = (
        P("dp", "row", "col"),
        P("row", ("dp", "col")),
        P("row", ("dp", "col")),
        P(None, "row", ("dp", "col")),
    )
    return jax.shard_map(
        shards,
        mesh=mesh,
        in_specs=placed,
        out_specs=(P(None, "row", ("dp", "col")), P("dp", "row", "col"), P("row", ("dp", "col"))),
        check_vma=False,
    )
```

```python
import jax
import jax.numpy as jnp
from jax import lax
from jax.experimental import pallas as pl
from jax.experimental.pallas import tpu as pltpu
from jax.sharding import PartitionSpec as P

inv_root_two = 0.7071067811865476
inv_root_two_pi = 0.3989422804014327
bf16, f32 = jnp.bfloat16, jnp.float32

NZ, NY, NX = 8, 4, 4
ROWS = 48
U = 16
D4 = 1920
H = 512
BW = 1024
BO = 896
GROUPS = ((0, 1), (1, 3), (3, 5), (5, 7), (7, 8))
NEAR = 3
DIRECT = 4
N_SEND, N_RECV = 208, 208


def pos_f(k):
    return 0 if k == 0 else 2 * k - 1


def pos_b(k):
    return 2 * k


def sib_pos(p):
    if p == 0 or p == 7:
        return p
    return p + 1 if p % 2 else p - 1


def gelu_pair(pre):
    normal_cdf = 0.5 * (1.0 + lax.erf(pre * inv_root_two))
    density = jnp.exp(-0.5 * pre * pre) * inv_root_two_pi
    return (pre * normal_cdf, normal_cdf + pre * density)


def kernel(inp, lev, scl, gh, hid, gin, gw,
           L, W, S0, R0, X, GH, HD, PS, PR, PM, GP, GI, GA, GW, CA, CB,
           A1s, Ass, A2s, A1r, Asr, A2r, YA,
           ZLs, ZLr, ZSs, ZSr, BLs, BLr, BSs, BSr, YB,
           Y1s, Yss, Y2s, Y1r, Ysr, Y2r, FA, FB, OA, OB,
           ssem, rsem, lsem):
    dp, x, col = lax.axis_index("dp"), lax.axis_index("row"), lax.axis_index("col")
    z, ylo, yhi, core = dp // 2, dp % 2, col // 2, col % 2
    y = 2 * yhi + ylo
    s = 1 - 2 * core

    def dev(zz, yy, xx, cc):
        return {"dp": zz * 2 + yy % 2, "row": xx, "col": (yy // 2) * 2 + cc}

    sources = [dev(z, 2 * (x // 2) + j, y, x % 2) for j in range(2)]
    targets = [dev(z, x, 2 * yhi + core, c) for c in range(2)]
    loops = (x == y) & (core == x % 2)
    z_f, z_b = dev((z + s + NZ) % NZ, y, x, core), dev((z - s + NZ) % NZ, y, x, core)
    y_f, y_b = dev(z, (y + s + NY) % NY, x, core), dev(z, (y - s + NY) % NY, x, core)
    sib = dev(z, y, x, 1 - core)
    y_2 = dev(z, (y + 2) % NY, x, core)
    x_f, x_b = dev(z, y, (x + s + NX) % NX, core), dev(z, y, (x - s + NX) % NX, core)
    x_2 = dev(z, y, (x + 2) % NX, core)
    xf1, xb1, xf2 = (x - s + NX) % NX, (x + s + NX) % NX, (x + 2) % NX
    yf1, yb1, yf2 = (y - s + NY) % NY, (y + s + NY) % NY, (y + 2) % NY

    sends, keys, sent = [], {}, [0]

    def rid(key):
        if key not in keys:
            keys[key] = len(keys)
        return rsem.at[keys[key]]

    def copy(src, dst, key, to):
        i = sent[0]
        sent[0] += 1
        return pltpu.make_async_remote_copy(src, dst, ssem.at[i], rid(key), device_id=to)

    def send(src, dst, key, to):
        c = copy(src, dst, key, to)
        c.start()
        sends.append(c)

    def arrived(dst, key):
        pltpu.make_async_remote_copy(dst, dst, ssem.at[0], rid(key), device_id=sib).wait_recv()

    lev_in = pltpu.make_async_copy(lev, L, lsem.at[0])
    gh_in = pltpu.make_async_copy(gh, GH, lsem.at[1])
    lev_in.start()
    gh_in.start()
    bar = pltpu.get_barrier_semaphore()
    partners = sources + targets + [x_f, x_b, x_2, z_f, z_b, y_f, y_b, y_2, sib]
    for d in partners:
        pl.semaphore_signal(bar, 1, device_id=d)
    block = inp[...].astype(f32)
    S0[...] = jnp.concatenate([block[:, :BW], block[:, BO:]], 0).astype(bf16)
    pl.semaphore_wait(bar, len(partners))

    rid(("swap",))
    i_swap = sent[0]
    sent[0] += 1
    to_chip = dev(z, x, 2 * yhi + core, ylo)
    swap = pltpu.make_async_remote_copy(S0, R0.at[ylo], ssem.at[i_swap], rid(("swap",)), device_id=to_chip)

    @pl.when(jnp.logical_not(loops))
    def _():
        swap.start()

    @pl.when(loops)
    def _():
        R0[core] = S0[...]

    def weights(a0, a1):
        @pl.loop(a0, a1)
        def _(a):
            r = pl.ds(pl.multiple_of(a * 128, 128), 128)
            for b in range(H // 128):
                cs = pl.ds(b * 128, 128)
                W[r, cs] = (L[r, cs].astype(f32) * scl[b, a]).astype(bf16)

    @pl.when(jnp.logical_not(loops))
    def _():
        arrived(R0.at[core], ("swap",))

    send(R0.at[core], R0.at[core], ("hand",), sib)
    lev_in.wait()
    weights(0, 8)
    arrived(R0.at[1 - core], ("hand",))
    pair = [jnp.concatenate([R0[j].astype(f32)[:24], R0[j].astype(f32)[24:, BW - BO:]], 1) for j in range(2)]
    X[y, 0] = jnp.concatenate(pair, 0).astype(bf16)

    r_mine = pl.ds(pl.multiple_of(core * U, U), U)
    r_other = pl.ds(pl.multiple_of((1 - core) * U, U), U)
    r_b = pl.ds(2 * U, U)
    c_mine = pl.ds(pl.multiple_of(core * BO, 128), BW)
    c_other = pl.ds(pl.multiple_of((1 - core) * BO, 128), BW)
    c_give = pl.ds(pl.multiple_of(core * BW, 128), BO)
    c_take = pl.ds(pl.multiple_of((1 - core) * BW, 128), BO)

    def a_unit(yq, p):
        return X.at[yq, p, r_mine]

    def b_unit(yq, p):
        return X.at[yq, p, r_b, c_mine]

    name_of = {id(y): "0", id(yf1): "f1", id(yb1): "b1", id(yf2): "f2"}

    def at_dist(k):
        return [0] if k == 0 else [pos_f(k)] + ([pos_b(k)] if k < 4 else [])

    def y_start(p):
        send(a_unit(y, p), a_unit(y, p), ("Ay", p, 1), y_f)
        send(a_unit(y, p), a_unit(y, p), ("Ay", p, -1), y_b)
        if p == 7:
            send(a_unit(y, p), a_unit(y, p), ("Ay", p, 2), y_2)

    def y_hop1(p):
        arrived(a_unit(yf1, p), ("Ay", p, 1))
        if p != 7:
            send(a_unit(yf1, p), a_unit(yf1, p), ("Ay", p, 2), y_f)
        if p == 0:
            send(a_unit(yf1, 0), a_unit(yf1, 0), ("As0", -1), sib)
        arrived(a_unit(yb1, p), ("Ay", p, -1))
        if p == 0:
            send(a_unit(yb1, 0), a_unit(yb1, 0), ("As0", 1), sib)

    def y_hop2(p):
        arrived(a_unit(yf2, p), ("Ay", p, 2))
        if p == 0:
            send(a_unit(yf2, 0), a_unit(yf2, 0), ("As0", 2), sib)
        else:
            send(X.at[:, p, r_mine], X.at[:, sib_pos(p), r_mine], ("As", sib_pos(p)), sib)

    def bz_send(yq, k):
        if k < 4:
            send(b_unit(yq, pos_f(k)), b_unit(yq, pos_f(k + 1)), ("Bz", name_of[id(yq)], pos_f(k + 1)), z_f)
        if k < 3:
            send(b_unit(yq, pos_b(k)), b_unit(yq, pos_b(k + 1)), ("Bz", name_of[id(yq)], pos_b(k + 1)), z_b)

    def bz_hop(yq, k):
        for p in at_dist(k):
            arrived(b_unit(yq, p), ("Bz", name_of[id(yq)], p))
        bz_send(yq, k)

    def b_give(k):
        for p in at_dist(k):
            send(X.at[:, p, r_b, c_give], X.at[:, sib_pos(p), r_b, c_give], ("Bs", sib_pos(p)), sib)

    def sib_wait(k):
        for p in at_dist(k):
            if p == 0:
                for q, yq in ((1, yf1), (-1, yb1), (2, yf2)):
                    arrived(X.at[yq, 0, r_other], ("As0", q))
                    arrived(X.at[yq, 0, r_b, c_take], ("Bs0", q))
            else:
                arrived(X.at[:, p, r_other], ("As", p))
                arrived(X.at[:, p, r_b, c_take], ("Bs", p))

    def az_send(k):
        if k < 4:
            send(a_unit(y, pos_f(k)), a_unit(y, pos_f(k + 1)), ("Az", pos_f(k + 1)), z_f)
        if k < 3:
            send(a_unit(y, pos_b(k)), a_unit(y, pos_b(k + 1)), ("Az", pos_b(k + 1)), z_b)

    def tick(k):
        if k == 0:
            az_send(0)
            for q, to in ((1, y_f), (-1, y_b), (2, y_2)):
                send(b_unit(y, 0), b_unit(y, 0), ("By", q), to)
            y_start(0)
            bz_send(y, 0)
            return
        if k <= 4:
            for p in at_dist(k):
                arrived(a_unit(y, p), ("Az", p))
            az_send(k)
            for p in at_dist(k):
                y_start(p)
        if k == 1:
            for q, yq, r in ((1, yf1, -1), (-1, yb1, 1), (2, yf2, 2)):
                arrived(b_unit(yq, 0), ("By", q))
                bz_send(yq, 0)
                send(X.at[yq, 0, r_b, c_give], X.at[yq, 0, r_b, c_give], ("Bs0", r), sib)
        if k <= 4:
            bz_hop(y, k)
        for p in at_dist(k - 1):
            y_hop1(p)
        if 2 <= k <= 5:
            for yq in (yf1, yb1, yf2):
                bz_hop(yq, k - 1)
            b_give(k - 1)
        if k >= 2:
            for p in at_dist(k - 2):
                y_hop2(p)
        if k == 5:
            y_hop2(7)

    def partial_pre(g):
        p0, p1 = GROUPS[g]
        m = (p1 - p0) * ROWS
        for h in range(0, H, 256):
            rows = X[:, p0:p1].reshape(NY * m, D4)
            part = jnp.dot(rows, W[:, h:h + 256], preferred_element_type=f32)
            PS[:, p0:p1, :, h:h + 256] = part.astype(bf16).reshape(NY, p1 - p0, ROWS, 256)
        send(PS.at[xf2, p0:p1], PR.at[0, p0:p1], ("pre", g, 0), x_2 if g >= DIRECT else x_b)
        send(PS.at[xb1, p0:p1], PR.at[1, p0:p1], ("pre", g, 1), x_f)
        if g >= DIRECT:
            send(PS.at[xf1, p0:p1], PR.at[2, p0:p1], ("pre", g, 2), x_b)

    def pre_middle(g):
        p0, p1 = GROUPS[g]
        arrived(PR.at[0, p0:p1], ("pre", g, 0))
        PM[p0:p1] = (PS[xf1, p0:p1].astype(f32) + PR[0, p0:p1].astype(f32)).astype(bf16)
        send(PM.at[p0:p1], PR.at[2, p0:p1], ("pre", g, 2), x_b)

    def activate(g):
        p0, p1 = GROUPS[g]
        parts = (0, 1, 2) if g >= DIRECT else (1, 2)
        for d in parts:
            arrived(PR.at[d, p0:p1], ("pre", g, d))

        @pl.loop(p0, p1)
        def _(p):
            k = (p + 1) // 2
            zz = (z + (1 - 2 * (p % 2)) * k * s + NZ) % NZ
            pre = PS[x, p].astype(f32)
            for d in parts:
                pre += PR[d, p].astype(f32)
            activated, slope = gelu_pair(pre)
            HD[zz] = activated.astype(bf16)
            GP[x, p] = (GH[zz].astype(f32) * slope).astype(bf16)

        own = GP.at[x, p0:p1]
        send(own, own, ("gp", g, 1), x_f)
        send(own, own, ("gp", g, -1), x_b)
        if g >= DIRECT:
            send(own, own, ("gp", g, 2), x_2)

    def grad_middle(g):
        p0, p1 = GROUPS[g]
        arrived(GP.at[xf1, p0:p1], ("gp", g, 1))
        send(GP.at[xf1, p0:p1], GP.at[xf1, p0:p1], ("gp", g, 2), x_f)

    def input_terms(g):
        p0, p1 = GROUPS[g]
        m = (p1 - p0) * ROWS
        if g >= DIRECT:
            arrived(GP.at[xf1, p0:p1], ("gp", g, 1))
        arrived(GP.at[xb1, p0:p1], ("gp", g, -1))
        arrived(GP.at[xf2, p0:p1], ("gp", g, 2))

        @pl.loop(0, D4 // 384)
        def _(n):
            cs = pl.ds(pl.multiple_of(n * 384, 128), 384)
            rows = GP[:, p0:p1].reshape(NY * m, H)
            part = lax.dot_general(rows, W[cs, :], (((1,), (1,)), ((), ())), preferred_element_type=f32)
            GI[:, p0:p1, :, cs] = part.astype(bf16).reshape(NY, p1 - p0, ROWS, 384)

        for p in reversed(range(p0, p1)):
            q = sib_pos(p)
            send(GI.at[:, p, r_b, c_other], CB.at[:, q], ("CB", q), sib)
            send(GI.at[:, p, r_other], CA.at[:, q], ("CA", q), sib)

    def a_term(yq, p):
        return GI[yq, p, r_mine].astype(f32) + CA[yq, p].astype(f32)

    def ay_begin(p):
        arrived(CA.at[:, p], ("CA", p))
        A1s[p] = a_term(yf2, p).astype(bf16)
        send(A1s.at[p], A1r.at[p], ("A1", p), y_2 if p == 7 else y_b)
        if p == 7:
            A2s[p] = a_term(yf1, p).astype(bf16)
            send(A2s.at[p], A2r.at[p], ("A2", p), y_b)
        Ass[p] = a_term(yb1, p).astype(bf16)
        send(Ass.at[p], Asr.at[p], ("As_", p), y_f)

    def ay_middle(p):
        arrived(A1r.at[p], ("A1", p))
        A2s[p] = (a_term(yf1, p) + A1r[p].astype(f32)).astype(bf16)
        send(A2s.at[p], A2r.at[p], ("A2", p), y_b)

    def ay_end(p):
        arrived(Asr.at[p], ("As_", p))
        arrived(A2r.at[p], ("A2", p))
        total = a_term(y, p) + Asr[p].astype(f32) + A2r[p].astype(f32)
        if p == 7:
            arrived(A1r.at[p], ("A1", p))
            total += A1r[p].astype(f32)
        YA[p] = total

    def z_chain(j, term, at, ls, lr, ss, sr, name):
        if j == 0:
            at(ls, 0)[...] = term(pos_f(4)).astype(bf16)
        else:
            arrived(at(lr, j - 1), (name, "L", j))
            if j < 4:
                at(ls, j)[...] = (term(pos_f(4 - j)) + at(lr, j - 1)[...].astype(f32)).astype(bf16)
        if j < 4:
            send(at(ls, j), at(lr, j), (name, "L", j + 1), z_b)
        if j == 0:
            at(ss, 0)[...] = term(pos_b(3)).astype(bf16)
        elif j < 4:
            arrived(at(sr, j - 1), (name, "S", j))
            if j < 3:
                at(ss, j)[...] = (term(pos_b(3 - j)) + at(sr, j - 1)[...].astype(f32)).astype(bf16)
        if j < 3:
            send(at(ss, j), at(sr, j), (name, "S", j + 1), z_f)
        if j == 4:
            return term(0) + at(lr, 3)[...].astype(f32) + at(sr, 2)[...].astype(f32)

    outs = []

    def start_out(c):
        c.start()
        outs.append(c)

    def hidden_out():
        start_out(pltpu.make_async_copy(HD, hid, lsem.at[2]))

    def weight_tile(n, p0, p1):
        cs = pl.ds(pl.multiple_of(n * 128, 128), 128)
        rows = X[:, p0:p1, :, cs].reshape(NY * (p1 - p0) * ROWS, 128)
        grads = GP[:, p0:p1].reshape(NY * (p1 - p0) * ROWS, H)
        return cs, lax.dot_general(rows, grads, (((0,), (0,)), ((), ())), preferred_element_type=f32)

    def weight_far(n0, n1):
        @pl.loop(n0, n1)
        def _(n):
            cs, part = weight_tile(n, NEAR, NZ)
            GA[cs, :] = part

    def weight_grad(n0, n1):
        @pl.loop(n0, n1)
        def _(n):
            cs, part = weight_tile(n, 0, NEAR)
            GW[cs, :] = (GA[cs, :] + part).astype(bf16)

        r = pl.ds(n0 * 128, (n1 - n0) * 128)
        start_out(pltpu.make_async_copy(GW.at[r], gw.at[r], lsem.at[3 + n0]))

    def b_step(j, *rows):
        for yq in rows:
            nm = name_of[id(yq)]
            last = z_chain(
                j,
                lambda p: GI[yq, p, r_b, c_mine].astype(f32) + CB[yq, p].astype(f32),
                lambda buf, i: buf.at[i, yq],
                BLs, BLr, BSs, BSr, "B" + nm,
            )
            if j < 4:
                continue
            YB[yq] = last
            if nm == "f2":
                Y1s[...] = last.astype(bf16)
                send(Y1s, Y1r, ("Y1",), y_2)
            elif nm == "f1":
                Y2s[...] = last.astype(bf16)
                send(Y2s, Y2r, ("Y2",), y_b)
            elif nm == "b1":
                Yss[...] = last.astype(bf16)
                send(Yss, Ysr, ("Ys",), y_f)

    def b_end():
        arrived(Ysr, ("Ys",))
        arrived(Y2r, ("Y2",))
        arrived(Y1r, ("Y1",))
        FB[...] = (YB[y] + Ysr[...].astype(f32) + Y2r[...].astype(f32) + Y1r[...].astype(f32)).astype(bf16)

    def cb_wait(*ps):
        for p in ps:
            arrived(CB.at[:, p], ("CB", p))

    def a_step(j):
        last = z_chain(j, lambda p: YA[p], lambda buf, i: buf.at[i], ZLs, ZLr, ZSs, ZSr, "A")
        if j == 4:
            FA[...] = last.astype(bf16)

    backs = []

    def give_back():
        always = core >= 0
        for j, src, dst, name, which in ((0, FA, OA, "OA", always), (1, FA, OA, "OA", core == 1), (1, FB, OB, "OB", always)):
            i = sent[0]
            sent[0] += 1
            rid((name, 0))
            rid((name, 1))
            sem = rsem.at[keys[(name, 0)] + core]
            which = which & jnp.logical_not(loops & (j == x % 2))
            backs.append((which, pltpu.make_async_remote_copy(src, dst.at[core], ssem.at[i], sem, device_id=sources[j])))
        for which, c in backs:

            @pl.when(which)
            def _():
                c.start()

        @pl.when(loops)
        def _():
            OA[core] = FA[...]
            OB[core] = FB[...]

    def take_back():
        for c in range(2):
            far = jnp.logical_not(loops & (core == c))

            @pl.when(far if c == 1 else far & (ylo == 0))
            def _():
                arrived(OA.at[c], ("OA", c))

            @pl.when(far & (ylo == 1))
            def _():
                arrived(OB.at[c], ("OB", c))

        a1 = OA[1].astype(f32)

        @pl.when(ylo == 0)
        def _():
            gin[...] = jnp.concatenate([OA[0].astype(f32), a1[:8]], 0).astype(bf16)

        @pl.when(ylo == 1)
        def _():
            last = jnp.concatenate([OB[0].astype(f32), OB[1].astype(f32)[:, 2 * BW - D4:]], 1)
            gin[...] = jnp.concatenate([a1[8:], last], 0).astype(bf16)

    steps = [
        (tick, 0), (weights, 8, 15), (gh_in.wait,),
        (tick, 1), (tick, 2),
        (sib_wait, 0), (partial_pre, 0),
        (tick, 3), (pre_middle, 0), (sib_wait, 1), (partial_pre, 1),
        (tick, 4), (activate, 0), (pre_middle, 1), (sib_wait, 2), (partial_pre, 2),
        (tick, 5), (grad_middle, 0), (pre_middle, 2),
        (sib_wait, 3), (partial_pre, 3), (sib_wait, 4), (partial_pre, 4),
        (input_terms, 0), (activate, 2), (pre_middle, 3), (activate, 4), (grad_middle, 2),
        (ay_begin, 0), (activate, 3), (activate, 1), (hidden_out,),
        (input_terms, 4), (grad_middle, 3), (ay_middle, 0),
        (input_terms, 2), (grad_middle, 1),
        (ay_begin, 7), (ay_begin, 3), (ay_begin, 4),
        (input_terms, 3),
        (ay_end, 0), (cb_wait, 7, 6, 5),
        (b_step, 0, yf2, yf1, yb1, y),
        (ay_begin, 5), (ay_begin, 6), (ay_end, 7), (ay_middle, 3), (ay_middle, 4),
        (weight_far, 0, 4),
        (input_terms, 1),
        (cb_wait, 4, 3),
        (b_step, 1, yf2, yf1, yb1, y),
        (ay_middle, 5), (ay_middle, 6), (ay_end, 3), (ay_end, 4),
        (weight_far, 4, 7),
        (cb_wait, 2, 1, 0),
        (ay_begin, 2), (ay_begin, 1),
        (b_step, 2, yf2, yf1, yb1, y),
        (ay_end, 6), (a_step, 0), (ay_end, 5),
        (weight_far, 7, 11),
        (ay_middle, 2), (ay_middle, 1),
        (a_step, 1),
        (b_step, 3, yf2, yf1, yb1, y),
        (weight_far, 11, 15),
        (ay_end, 2), (a_step, 2), (ay_end, 1),
        (b_step, 4, yf2, yf1, yb1, y),
        (weight_grad, 0, 4),
        (a_step, 3),
        (weight_grad, 4, 8),
        (b_end,),
        (a_step, 4),
        (give_back,),
        (weight_grad, 8, 15),
        (take_back,),
    ]
    for step, *args in steps:
        step(*args)

    @pl.when(jnp.logical_not(loops))
    def _():
        swap.wait_send()

    for which, c in backs:

        @pl.when(which)
        def _():
            c.wait_send()

    for c in sends:
        c.wait_send()
    for c in outs:
        c.wait()
    assert sent[0] <= N_SEND and len(keys) <= N_RECV, (sent, len(keys))


def flush(h, i, w, ho, io, wo, sem):
    cut = [pl.ds(n * (D4 // 4), D4 // 4) for n in range(4)]
    parts = [(w.at[r], wo.at[r]) for r in cut] + [(h, ho), (i, io)]
    copies = [pltpu.make_async_copy(a, o, sem.at[n]) for n, (a, o) in enumerate(parts)]
    for c in copies:
        c.start()
    for c in copies:
        c.wait()


def shards(inputs, levels, block_scales, grad_hidden):
    vm = lambda *shape: pltpu.VMEM(shape, bf16)
    vf = lambda *shape: pltpu.VMEM(shape, f32)
    vmem, smem = pl.BlockSpec(memory_space=pltpu.VMEM), pl.BlockSpec(memory_space=pltpu.SMEM)
    hbm, far = pl.BlockSpec(memory_space=pl.ANY), pl.BlockSpec(memory_space=pltpu.HBM)
    stay = lambda a: pltpu.with_memory_space_constraint(a, pltpu.HBM)
    a_buf = vm(NZ, U, D4)
    y_buf = vm(U, BW)
    out_shape = (
        jax.ShapeDtypeStruct((NZ, ROWS, H), bf16),
        jax.ShapeDtypeStruct((24, D4), bf16),
        jax.ShapeDtypeStruct((D4, H), bf16),
    )
    outs = pl.pallas_call(
        kernel,
        out_shape=out_shape,
        in_specs=[vmem, far, smem, far],
        out_specs=(hbm, vmem, hbm),
        scratch_shapes=[
            vm(D4, H), vm(D4, H),
            vm(ROWS, BW), vm(2, ROWS, BW),
            vm(NY, NZ, ROWS, D4),
            vm(NZ, ROWS, H), vm(NZ, ROWS, H),
            vm(NY, NZ, ROWS, H), vm(NX - 1, NZ, ROWS, H), vm(NZ, ROWS, H), vm(NY, NZ, ROWS, H),
            vm(NY, NZ, ROWS, D4), vf(D4, H), vm(D4, H),
            vm(NY, NZ, U, D4), vm(NY, NZ, U, BW),
            a_buf, a_buf, a_buf, a_buf, a_buf, a_buf, vf(NZ, U, D4),
            vm(4, U, D4), vm(4, U, D4), vm(3, U, D4), vm(3, U, D4),
            vm(4, NY, U, BW), vm(4, NY, U, BW), vm(3, NY, U, BW), vm(3, NY, U, BW), vf(NY, U, BW),
            y_buf, y_buf, y_buf, y_buf, y_buf, y_buf,
            vm(U, D4), y_buf, vm(2, U, D4), vm(2, U, BW),
            pltpu.SemaphoreType.DMA((N_SEND,)),
            pltpu.SemaphoreType.DMA((N_RECV,)),
            pltpu.SemaphoreType.DMA((20,)),
        ],
        compiler_params=pltpu.CompilerParams(
            collective_id=0, has_side_effects=True, vmem_limit_bytes=46 * 2**20
        ),
        name="grid_layer",
    )(inputs[0], stay(levels), block_scales.T, stay(grad_hidden.reshape(NZ, ROWS, H)))
    hidden, grad_inputs, grad_weight = pl.pallas_call(
        flush,
        out_shape=out_shape,
        in_specs=[hbm] * 3,
        out_specs=(hbm,) * 3,
        scratch_shapes=[pltpu.SemaphoreType.DMA((6,))],
        compiler_params=pltpu.CompilerParams(vmem_limit_bytes=2**20),
        name="flush",
    )(*outs)
    return (hidden.reshape(grad_hidden.shape), grad_inputs[None], grad_weight)


def solution(mesh):
    placed = (
        P("dp", "row", "col"),
        P("row", ("dp", "col")),
        P("row", ("dp", "col")),
        P(None, "row", ("dp", "col")),
    )
    return jax.shard_map(
        shards,
        mesh=mesh,
        in_specs=placed,
        out_specs=(P(None, "row", ("dp", "col")), P("dp", "row", "col"), P("row", ("dp", "col"))),
        check_vma=False,
    )
```

```python
import jax
import jax.numpy as jnp
from jax import lax
from jax.experimental import pallas as pl
from jax.experimental.pallas import tpu as pltpu
from jax.sharding import PartitionSpec as P

inv_root_two = 0.7071067811865476
inv_root_two_pi = 0.3989422804014327
bf16, f32 = jnp.bfloat16, jnp.float32

NZ, NY, NX = 8, 4, 4
ROWS = 48
U = 16
D4 = 1920
H = 512
BW = 1024
BO = 896
GROUPS = ((0, 1), (1, 3), (3, 5), (5, 7), (7, 8))
NEAR = 3
DIRECT = 4
N_SEND, N_RECV = 208, 208


def pos_f(k):
    return 0 if k == 0 else 2 * k - 1


def pos_b(k):
    return 2 * k


def sib_pos(p):
    if p == 0 or p == 7:
        return p
    return p + 1 if p % 2 else p - 1


def gelu_pair(pre):
    normal_cdf = 0.5 * (1.0 + lax.erf(pre * inv_root_two))
    density = jnp.exp(-0.5 * pre * pre) * inv_root_two_pi
    return (pre * normal_cdf, normal_cdf + pre * density)


def kernel(inp, lev, scl_hbm, gh, hid, gin, gw,
           B0, scl, L, W, WT, S0, R0, X, GH, HD, PS, PR, PM, GP, GI, GA, GW, CA, CB,
           A1s, Ass, A2s, A1r, Asr, A2r, YA,
           ZLs, ZLr, ZSs, ZSr, BLs, BLr, BSs, BSr, YB,
           Y1s, Yss, Y2s, Y1r, Ysr, Y2r, FA, FB, OA, OB,
           ssem, rsem, lsem):
    dp, x, col = lax.axis_index("dp"), lax.axis_index("row"), lax.axis_index("col")
    z, ylo, yhi, core = dp // 2, dp % 2, col // 2, col % 2
    y = 2 * yhi + ylo
    s = 1 - 2 * core

    def dev(zz, yy, xx, cc):
        return {"dp": zz * 2 + yy % 2, "row": xx, "col": (yy // 2) * 2 + cc}

    sources = [dev(z, 2 * (x // 2) + j, y, x % 2) for j in range(2)]
    targets = [dev(z, x, 2 * yhi + core, c) for c in range(2)]
    loops = (x == y) & (core == x % 2)
    z_f, z_b = dev((z + s + NZ) % NZ, y, x, core), dev((z - s + NZ) % NZ, y, x, core)
    y_f, y_b = dev(z, (y + s + NY) % NY, x, core), dev(z, (y - s + NY) % NY, x, core)
    sib = dev(z, y, x, 1 - core)
    y_2 = dev(z, (y + 2) % NY, x, core)
    x_f, x_b = dev(z, y, (x + s + NX) % NX, core), dev(z, y, (x - s + NX) % NX, core)
    x_2 = dev(z, y, (x + 2) % NX, core)
    xf1, xb1, xf2 = (x - s + NX) % NX, (x + s + NX) % NX, (x + 2) % NX
    yf1, yb1, yf2 = (y - s + NY) % NY, (y + s + NY) % NY, (y + 2) % NY

    sends, keys, sent = [], {}, [0]

    def rid(key):
        if key not in keys:
            keys[key] = len(keys)
        return rsem.at[keys[key]]

    def copy(src, dst, key, to):
        i = sent[0]
        sent[0] += 1
        return pltpu.make_async_remote_copy(src, dst, ssem.at[i], rid(key), device_id=to)

    def send(src, dst, key, to):
        c = copy(src, dst, key, to)
        c.start()
        sends.append(c)

    def arrived(dst, key):
        pltpu.make_async_remote_copy(dst, dst, ssem.at[0], rid(key), device_id=sib).wait_recv()

    in_c = pltpu.make_async_copy(inp, B0, lsem.at[18])
    scl_in = pltpu.make_async_copy(scl_hbm, scl, lsem.at[19])
    lev_in = pltpu.make_async_copy(lev, L, lsem.at[0])
    gh_in = pltpu.make_async_copy(gh, GH, lsem.at[1])
    in_c.start()
    scl_in.start()
    lev_in.start()
    gh_in.start()
    bar = pltpu.get_barrier_semaphore()
    partners = sources + targets + [x_f, x_b, x_2, z_f, z_b, y_f, y_b, y_2, sib]
    for d in partners:
        pl.semaphore_signal(bar, 1, device_id=d)
    in_c.wait()
    block = B0[...].astype(f32)
    S0[...] = jnp.concatenate([block[:, :BW], block[:, BO:]], 0).astype(bf16)
    pl.semaphore_wait(bar, len(partners))

    rid(("swap",))
    i_swap = sent[0]
    sent[0] += 1
    to_chip = dev(z, x, 2 * yhi + core, ylo)
    swap = pltpu.make_async_remote_copy(S0, R0.at[ylo], ssem.at[i_swap], rid(("swap",)), device_id=to_chip)

    @pl.when(jnp.logical_not(loops))
    def _():
        swap.start()

    @pl.when(loops)
    def _():
        R0[core] = S0[...]

    def weights(a0, a1):
        @pl.loop(a0, a1)
        def _(a):
            r = pl.ds(pl.multiple_of(a * 128, 128), 128)
            for b in range(H // 128):
                cs = pl.ds(b * 128, 128)
                block = L[r, cs].astype(f32) * scl[b, a]
                W[r, cs] = block.astype(bf16)
                WT[cs, r] = block.T.astype(bf16)

    @pl.when(jnp.logical_not(loops))
    def _():
        arrived(R0.at[core], ("swap",))

    send(R0.at[core], R0.at[core], ("hand",), sib)

    def unpacked(j):
        both = R0[j].astype(f32)
        return jnp.concatenate([both[:24], both[24:, BW - BO:]], 1)

    def put_a(c):
        X[y, 0, 2 * U * c:2 * U * c + U] = unpacked(c)[8 * c:8 * c + U].astype(bf16)

    for c in range(2):

        @pl.when(core == c)
        def _():
            put_a(c)

    def rest():
        scl_in.wait()
        lev_in.wait()
        weights(0, 5)
        arrived(R0.at[1 - core], ("hand",))
        X[y, 0, U:2 * U] = jnp.concatenate([unpacked(0)[U:], unpacked(1)[:8]], 0).astype(bf16)
        for c in range(2):

            @pl.when(core == 1 - c)
            def _():
                put_a(c)

    r_mine = pl.ds(pl.multiple_of(core * 2 * U, U), U)
    r_other = pl.ds(pl.multiple_of((1 - core) * 2 * U, U), U)
    r_b = pl.ds(U, U)
    c_mine = pl.ds(pl.multiple_of(core * BO, 128), BW)
    c_other = pl.ds(pl.multiple_of((1 - core) * BO, 128), BW)
    c_give = pl.ds(pl.multiple_of(core * BW, 128), BO)
    c_take = pl.ds(pl.multiple_of((1 - core) * BW, 128), BO)

    def a_unit(yq, p):
        return X.at[yq, p, r_mine]

    def b_unit(yq, p):
        return X.at[yq, p, r_b, c_mine]

    name_of = {id(y): "0", id(yf1): "f1", id(yb1): "b1", id(yf2): "f2"}

    def at_dist(k):
        return [0] if k == 0 else [pos_f(k)] + ([pos_b(k)] if k < 4 else [])

    def y_start(p):
        send(a_unit(y, p), a_unit(y, p), ("Ay", p, 1), y_f)
        send(a_unit(y, p), a_unit(y, p), ("Ay", p, -1), y_b)
        if p == 7:
            send(a_unit(y, p), a_unit(y, p), ("Ay", p, 2), y_2)

    def y_hop1(p):
        arrived(a_unit(yf1, p), ("Ay", p, 1))
        if p != 7:
            send(a_unit(yf1, p), a_unit(yf1, p), ("Ay", p, 2), y_f)
        if p == 0:
            send(a_unit(yf1, 0), a_unit(yf1, 0), ("As0", -1), sib)
        arrived(a_unit(yb1, p), ("Ay", p, -1))
        if p == 0:
            send(a_unit(yb1, 0), a_unit(yb1, 0), ("As0", 1), sib)

    def y_hop2(p):
        arrived(a_unit(yf2, p), ("Ay", p, 2))
        if p == 0:
            send(a_unit(yf2, 0), a_unit(yf2, 0), ("As0", 2), sib)
        else:
            send(X.at[:, p, r_mine], X.at[:, sib_pos(p), r_mine], ("As", sib_pos(p)), sib)

    def bz_send(yq, k):
        if k < 4:
            send(b_unit(yq, pos_f(k)), b_unit(yq, pos_f(k + 1)), ("Bz", name_of[id(yq)], pos_f(k + 1)), z_f)
        if k < 3:
            send(b_unit(yq, pos_b(k)), b_unit(yq, pos_b(k + 1)), ("Bz", name_of[id(yq)], pos_b(k + 1)), z_b)

    def bz_hop(yq, k):
        for p in at_dist(k):
            arrived(b_unit(yq, p), ("Bz", name_of[id(yq)], p))
        bz_send(yq, k)

    def b_give(k):
        for p in at_dist(k):
            send(X.at[:, p, r_b, c_give], X.at[:, sib_pos(p), r_b, c_give], ("Bs", sib_pos(p)), sib)

    def sib_wait(k):
        for p in at_dist(k):
            if p == 0:
                for q, yq in ((1, yf1), (-1, yb1), (2, yf2)):
                    arrived(X.at[yq, 0, r_other], ("As0", q))
                    arrived(X.at[yq, 0, r_b, c_take], ("Bs0", q))
            else:
                arrived(X.at[:, p, r_other], ("As", p))
                arrived(X.at[:, p, r_b, c_take], ("Bs", p))

    def az_send(k):
        if k < 4:
            send(a_unit(y, pos_f(k)), a_unit(y, pos_f(k + 1)), ("Az", pos_f(k + 1)), z_f)
        if k < 3:
            send(a_unit(y, pos_b(k)), a_unit(y, pos_b(k + 1)), ("Az", pos_b(k + 1)), z_b)

    def tick(k):
        if k == 0:
            az_send(0)
            y_start(0)
            rest()
            for q, to in ((1, y_f), (-1, y_b), (2, y_2)):
                send(b_unit(y, 0), b_unit(y, 0), ("By", q), to)
            bz_send(y, 0)
            return
        if k <= 4:
            for p in at_dist(k):
                arrived(a_unit(y, p), ("Az", p))
            az_send(k)
            for p in at_dist(k):
                y_start(p)
        if k == 1:
            for q, yq, r in ((1, yf1, -1), (-1, yb1, 1), (2, yf2, 2)):
                arrived(b_unit(yq, 0), ("By", q))
                bz_send(yq, 0)
                send(X.at[yq, 0, r_b, c_give], X.at[yq, 0, r_b, c_give], ("Bs0", r), sib)
        if k <= 4:
            bz_hop(y, k)
        for p in at_dist(k - 1):
            y_hop1(p)
        if 2 <= k <= 5:
            for yq in (yf1, yb1, yf2):
                bz_hop(yq, k - 1)
            b_give(k - 1)
        if k >= 2:
            for p in at_dist(k - 2):
                y_hop2(p)
        if k == 5:
            y_hop2(7)

    def partial_pre(g):
        p0, p1 = GROUPS[g]
        m = (p1 - p0) * ROWS
        for h in range(0, H, 256):
            rows = X[:, p0:p1].reshape(NY * m, D4)
            part = jnp.dot(rows, W[:, h:h + 256], preferred_element_type=f32)
            PS[:, p0:p1, :, h:h + 256] = part.astype(bf16).reshape(NY, p1 - p0, ROWS, 256)
        send(PS.at[xf2, p0:p1], PR.at[0, p0:p1], ("pre", g, 0), x_2 if g >= DIRECT else x_b)
        send(PS.at[xb1, p0:p1], PR.at[1, p0:p1], ("pre", g, 1), x_f)
        if g >= DIRECT:
            send(PS.at[xf1, p0:p1], PR.at[2, p0:p1], ("pre", g, 2), x_b)

    def pre_middle(g):
        p0, p1 = GROUPS[g]
        arrived(PR.at[0, p0:p1], ("pre", g, 0))
        PM[p0:p1] = (PS[xf1, p0:p1].astype(f32) + PR[0, p0:p1].astype(f32)).astype(bf16)
        send(PM.at[p0:p1], PR.at[2, p0:p1], ("pre", g, 2), x_b)

    def activate(g):
        p0, p1 = GROUPS[g]
        parts = (0, 1, 2) if g >= DIRECT else (1, 2)
        for d in parts:
            arrived(PR.at[d, p0:p1], ("pre", g, d))

        @pl.loop(p0, p1)
        def _(p):
            k = (p + 1) // 2
            zz = (z + (1 - 2 * (p % 2)) * k * s + NZ) % NZ
            pre = PS[x, p].astype(f32)
            for d in parts:
                pre += PR[d, p].astype(f32)
            activated, slope = gelu_pair(pre)
            HD[zz] = activated.astype(bf16)
            GP[x, p] = (GH[zz].astype(f32) * slope).astype(bf16)

        own = GP.at[x, p0:p1]
        send(own, own, ("gp", g, 1), x_f)
        send(own, own, ("gp", g, -1), x_b)
        if g >= DIRECT:
            send(own, own, ("gp", g, 2), x_2)

    def grad_middle(g):
        p0, p1 = GROUPS[g]
        arrived(GP.at[xf1, p0:p1], ("gp", g, 1))
        send(GP.at[xf1, p0:p1], GP.at[xf1, p0:p1], ("gp", g, 2), x_f)

    def input_terms(g):
        p0, p1 = GROUPS[g]
        m = (p1 - p0) * ROWS
        if g >= DIRECT:
            arrived(GP.at[xf1, p0:p1], ("gp", g, 1))
        arrived(GP.at[xb1, p0:p1], ("gp", g, -1))
        arrived(GP.at[xf2, p0:p1], ("gp", g, 2))

        @pl.loop(0, D4 // 384)
        def _(n):
            cs = pl.ds(pl.multiple_of(n * 384, 128), 384)
            rows = GP[:, p0:p1].reshape(NY * m, H)
            part = jnp.dot(rows, WT[:, cs], preferred_element_type=f32)
            GI[:, p0:p1, :, cs] = part.astype(bf16).reshape(NY, p1 - p0, ROWS, 384)

        for p in reversed(range(p0, p1)):
            q = sib_pos(p)
            send(GI.at[:, p, r_b, c_other], CB.at[:, q], ("CB", q), sib)
            send(GI.at[:, p, r_other], CA.at[:, q], ("CA", q), sib)

    def a_term(yq, p):
        return GI[yq, p, r_mine].astype(f32) + CA[yq, p].astype(f32)

    def ay_begin(p):
        arrived(CA.at[:, p], ("CA", p))
        A1s[p] = a_term(yf2, p).astype(bf16)
        send(A1s.at[p], A1r.at[p], ("A1", p), y_2 if p >= 5 else y_b)
        if p >= 5:
            A2s[p] = a_term(yf1, p).astype(bf16)
            send(A2s.at[p], A2r.at[p], ("A2", p), y_b)
        Ass[p] = a_term(yb1, p).astype(bf16)
        send(Ass.at[p], Asr.at[p], ("As_", p), y_f)

    def ay_middle(p):
        arrived(A1r.at[p], ("A1", p))
        A2s[p] = (a_term(yf1, p) + A1r[p].astype(f32)).astype(bf16)
        send(A2s.at[p], A2r.at[p], ("A2", p), y_b)

    def ay_end(p):
        arrived(Asr.at[p], ("As_", p))
        arrived(A2r.at[p], ("A2", p))
        total = a_term(y, p) + Asr[p].astype(f32) + A2r[p].astype(f32)
        if p >= 5:
            arrived(A1r.at[p], ("A1", p))
            total += A1r[p].astype(f32)
        YA[p] = total

    def z_chain(j, term, at, ls, lr, ss, sr, name):
        if j == 0:
            at(ls, 0)[...] = term(pos_f(4)).astype(bf16)
        else:
            arrived(at(lr, j - 1), (name, "L", j))
            if j < 4:
                at(ls, j)[...] = (term(pos_f(4 - j)) + at(lr, j - 1)[...].astype(f32)).astype(bf16)
        if j < 4:
            send(at(ls, j), at(lr, j), (name, "L", j + 1), z_b)
        if j == 0:
            at(ss, 0)[...] = term(pos_b(3)).astype(bf16)
        elif j < 4:
            arrived(at(sr, j - 1), (name, "S", j))
            if j < 3:
                at(ss, j)[...] = (term(pos_b(3 - j)) + at(sr, j - 1)[...].astype(f32)).astype(bf16)
        if j < 3:
            send(at(ss, j), at(sr, j), (name, "S", j + 1), z_f)
        if j == 4:
            return term(0) + at(lr, 3)[...].astype(f32) + at(sr, 2)[...].astype(f32)

    outs = []

    def start_out(c):
        c.start()
        outs.append(c)

    def hidden_out():
        start_out(pltpu.make_async_copy(HD, hid, lsem.at[2]))

    def weight_tile(n, p0, p1):
        cs = pl.ds(pl.multiple_of(n * 128, 128), 128)
        rows = X[:, p0:p1, :, cs].reshape(NY * (p1 - p0) * ROWS, 128)
        grads = GP[:, p0:p1].reshape(NY * (p1 - p0) * ROWS, H)
        return cs, lax.dot_general(rows, grads, (((0,), (0,)), ((), ())), preferred_element_type=f32)

    def weight_far(n0, n1):
        @pl.loop(n0, n1)
        def _(n):
            cs, part = weight_tile(n, NEAR, NZ)
            GA[cs, :] = part

    def weight_grad(n0, n1):
        @pl.loop(n0, n1)
        def _(n):
            cs, part = weight_tile(n, 0, NEAR)
            GW[cs, :] = (GA[cs, :] + part).astype(bf16)

        r = pl.ds(n0 * 128, (n1 - n0) * 128)
        start_out(pltpu.make_async_copy(GW.at[r], gw.at[r], lsem.at[3 + n0]))

    def b_step(j, *rows):
        for yq in rows:
            nm = name_of[id(yq)]
            last = z_chain(
                j,
                lambda p: GI[yq, p, r_b, c_mine].astype(f32) + CB[yq, p].astype(f32),
                lambda buf, i: buf.at[i, yq],
                BLs, BLr, BSs, BSr, "B" + nm,
            )
            if j < 4:
                continue
            YB[yq] = last
            if nm == "f2":
                Y1s[...] = last.astype(bf16)
                send(Y1s, Y1r, ("Y1",), y_2)
            elif nm == "f1":
                Y2s[...] = last.astype(bf16)
                send(Y2s, Y2r, ("Y2",), y_b)
            elif nm == "b1":
                Yss[...] = last.astype(bf16)
                send(Yss, Ysr, ("Ys",), y_f)

    def b_end():
        arrived(Ysr, ("Ys",))
        arrived(Y2r, ("Y2",))
        arrived(Y1r, ("Y1",))
        FB[...] = (YB[y] + Ysr[...].astype(f32) + Y2r[...].astype(f32) + Y1r[...].astype(f32)).astype(bf16)

    def cb_wait(*ps):
        for p in ps:
            arrived(CB.at[:, p], ("CB", p))

    def a_step(j):
        last = z_chain(j, lambda p: YA[p], lambda buf, i: buf.at[i], ZLs, ZLr, ZSs, ZSr, "A")
        if j == 4:
            FA[...] = last.astype(bf16)

    backs = []
    rid(("OB", 0))
    rid(("OB", 1))
    b_sems = keys[("OB", 0)]

    def give_back():
        for j in range(2):
            other = jnp.logical_not(loops & (j == x % 2))
            for src, dst, sem, which in (
                (FA, OA, rid(("OA",)), other & (core == j)),
                (FB, OB.at[core], rsem.at[b_sems + core], other),
            ):
                i = sent[0]
                sent[0] += 1
                backs.append((which, pltpu.make_async_remote_copy(src, dst, ssem.at[i], sem, device_id=sources[j])))
        for which, c in backs:

            @pl.when(which)
            def _():
                c.start()

        @pl.when(loops)
        def _():
            OA[...] = FA[...]
            OB[core] = FB[...]

    def take_back():
        @pl.when(jnp.logical_not(loops))
        def _():
            arrived(OA, ("OA",))

        for c in range(2):

            @pl.when(jnp.logical_not(loops & (core == c)))
            def _():
                arrived(OB.at[c], ("OB", c))

        a_rows = OA[...].astype(f32)
        b_rows = jnp.concatenate([OB[0].astype(f32), OB[1].astype(f32)[:, 2 * BW - D4:]], 1)

        @pl.when(ylo == 0)
        def _():
            gin[...] = jnp.concatenate([a_rows, b_rows[:8]], 0).astype(bf16)

        @pl.when(ylo == 1)
        def _():
            gin[...] = jnp.concatenate([b_rows[8:], a_rows], 0).astype(bf16)

    steps = [
        (tick, 0), (weights, 5, 15), (gh_in.wait,),
        (tick, 1), (tick, 2),
        (sib_wait, 0), (partial_pre, 0),
        (tick, 3), (pre_middle, 0), (sib_wait, 1), (partial_pre, 1),
        (tick, 4), (activate, 0), (sib_wait, 2), (partial_pre, 2),
        (tick, 5), (pre_middle, 1), (grad_middle, 0),
        (sib_wait, 3), (partial_pre, 3), (sib_wait, 4), (partial_pre, 4),
        (pre_middle, 2), (input_terms, 0), (activate, 2), (pre_middle, 3), (activate, 4), (grad_middle, 2),
        (ay_begin, 0), (activate, 3), (activate, 1), (hidden_out,),
        (input_terms, 4), (grad_middle, 3), (ay_middle, 0),
        (input_terms, 2), (grad_middle, 1),
        (ay_begin, 7), (ay_begin, 3), (ay_begin, 4),
        (input_terms, 3),
        (ay_end, 0), (cb_wait, 7, 6, 5),
        (b_step, 0, yf2, yf1, yb1, y),
        (ay_begin, 6), (ay_begin, 5), (ay_end, 7), (ay_middle, 3), (ay_middle, 4),
        (input_terms, 1),
        (cb_wait, 4, 3),
        (b_step, 1, yf2, yf1, yb1, y),
        (ay_end, 6), (a_step, 0), (ay_end, 5),
        (cb_wait, 2, 1, 0), (ay_begin, 2), (ay_begin, 1), (ay_end, 4), (ay_end, 3),
        (weight_far, 0, 3),
        (b_step, 2, yf2, yf1, yb1, y),
        (a_step, 1),
        (weight_far, 3, 6),
        (ay_middle, 2), (ay_middle, 1),
        (b_step, 3, yf2, yf1, yb1, y),
        (ay_end, 2), (a_step, 2), (ay_end, 1),
        (weight_far, 6, 10),
        (b_step, 4, yf2, yf1, yb1, y),
        (weight_far, 10, 12),
        (a_step, 3),
        (weight_far, 12, 15), (weight_grad, 0, 5),
        (b_end,),
        (a_step, 4),
        (give_back,),
        (weight_grad, 5, 15),
        (take_back,),
    ]
    for step, *args in steps:
        step(*args)

    @pl.when(jnp.logical_not(loops))
    def _():
        swap.wait_send()

    for which, c in backs:

        @pl.when(which)
        def _():
            c.wait_send()

    for c in sends:
        c.wait_send()
    for c in outs:
        c.wait()
    assert sent[0] <= N_SEND and len(keys) <= N_RECV, (sent, len(keys))


def flush(h, i, w, ho, io, wo, sem):
    cut = [pl.ds(n * (D4 // 4), D4 // 4) for n in range(4)]
    parts = [(w.at[r], wo.at[r]) for r in cut] + [(h, ho), (i, io)]
    copies = [pltpu.make_async_copy(a, o, sem.at[n]) for n, (a, o) in enumerate(parts)]
    for c in copies:
        c.start()
    for c in copies:
        c.wait()


def shards(inputs, levels, block_scales, grad_hidden):
    vm = lambda *shape: pltpu.VMEM(shape, bf16)
    vf = lambda *shape: pltpu.VMEM(shape, f32)
    vmem = pl.BlockSpec(memory_space=pltpu.VMEM)
    hbm, far = pl.BlockSpec(memory_space=pl.ANY), pl.BlockSpec(memory_space=pltpu.HBM)
    stay = lambda a: pltpu.with_memory_space_constraint(a, pltpu.HBM)
    a_buf = vm(NZ, U, D4)
    y_buf = vm(U, BW)
    out_shape = (
        jax.ShapeDtypeStruct((NZ, ROWS, H), bf16),
        jax.ShapeDtypeStruct((24, D4), bf16),
        jax.ShapeDtypeStruct((D4, H), bf16),
    )
    outs = pl.pallas_call(
        kernel,
        out_shape=out_shape,
        in_specs=[far, far, far, far],
        out_specs=(hbm, vmem, hbm),
        scratch_shapes=[
            vm(24, D4), pltpu.SMEM((H // 128, D4 // 128), f32),
            vm(D4, H), vm(D4, H), vm(H, D4),
            vm(ROWS, BW), vm(2, ROWS, BW),
            vm(NY, NZ, ROWS, D4),
            vm(NZ, ROWS, H), vm(NZ, ROWS, H),
            vm(NY, NZ, ROWS, H), vm(NX - 1, NZ, ROWS, H), vm(NZ, ROWS, H), vm(NY, NZ, ROWS, H),
            vm(NY, NZ, ROWS, D4), vf(D4, H), vm(D4, H),
            vm(NY, NZ, U, D4), vm(NY, NZ, U, BW),
            a_buf, a_buf, a_buf, a_buf, a_buf, a_buf, vf(NZ, U, D4),
            vm(4, U, D4), vm(4, U, D4), vm(3, U, D4), vm(3, U, D4),
            vm(4, NY, U, BW), vm(4, NY, U, BW), vm(3, NY, U, BW), vm(3, NY, U, BW), vf(NY, U, BW),
            y_buf, y_buf, y_buf, y_buf, y_buf, y_buf,
            vm(U, D4), y_buf, vm(U, D4), vm(2, U, BW),
            pltpu.SemaphoreType.DMA((N_SEND,)),
            pltpu.SemaphoreType.DMA((N_RECV,)),
            pltpu.SemaphoreType.DMA((24,)),
        ],
        compiler_params=pltpu.CompilerParams(
            collective_id=0, has_side_effects=True, vmem_limit_bytes=46 * 2**20
        ),
        name="grid_layer",
    )(stay(inputs[0]), stay(levels), stay(block_scales.T), stay(grad_hidden.reshape(NZ, ROWS, H)))
    hidden, grad_inputs, grad_weight = pl.pallas_call(
        flush,
        out_shape=out_shape,
        in_specs=[hbm] * 3,
        out_specs=(hbm,) * 3,
        scratch_shapes=[pltpu.SemaphoreType.DMA((6,))],
        compiler_params=pltpu.CompilerParams(vmem_limit_bytes=2**20),
        name="flush",
    )(*outs)
    return (hidden.reshape(grad_hidden.shape), grad_inputs[None], grad_weight)


def solution(mesh):
    placed = (
        P("dp", "row", "col"),
        P("row", ("dp", "col")),
        P("row", ("dp", "col")),
        P(None, "row", ("dp", "col")),
    )
    return jax.shard_map(
        shards,
        mesh=mesh,
        in_specs=placed,
        out_specs=(P(None, "row", ("dp", "col")), P("dp", "row", "col"), P("row", ("dp", "col"))),
        check_vma=False,
    )
```

```python
import jax
import jax.numpy as jnp
from jax import lax
from jax.experimental import pallas as pl
from jax.experimental.pallas import tpu as pltpu
from jax.sharding import PartitionSpec as P

inv_root_two = 0.7071067811865476
inv_root_two_pi = 0.3989422804014327
bf16, f32 = jnp.bfloat16, jnp.float32

NZ, NY, NX = 8, 4, 4
ROWS = 48
U = 16
D4 = 1920
H = 512
BW = 1024
BO = 896
GROUPS = ((0, 1), (1, 3), (3, 5), (5, 7), (7, 8))
NEAR = 3
DIRECT = 4
N_SEND, N_RECV = 208, 208


def pos_f(k):
    return 0 if k == 0 else 2 * k - 1


def pos_b(k):
    return 2 * k


def sib_pos(p):
    if p == 0 or p == 7:
        return p
    return p + 1 if p % 2 else p - 1


def gelu_pair(pre):
    normal_cdf = 0.5 * (1.0 + lax.erf(pre * inv_root_two))
    density = jnp.exp(-0.5 * pre * pre) * inv_root_two_pi
    return (pre * normal_cdf, normal_cdf + pre * density)


def kernel(inp, lev, scl_hbm, gh, hid, gin, gw,
           B0, scl, L, W, WT, SA, SB, RB, X, GH, HD, PS, PR, PM, GP, GI, GA, GW, CA, CB,
           A1s, Ass, A2s, A1r, Asr, A2r, YA,
           ZLs, ZLr, ZSs, ZSr, BLs, BLr, BSs, BSr, YB,
           Y1s, Yss, Y2s, Y1r, Ysr, Y2r, FA, FB, OA, OB,
           ssem, rsem, lsem):
    dp, x, col = lax.axis_index("dp"), lax.axis_index("row"), lax.axis_index("col")
    z, ylo, yhi, core = dp // 2, dp % 2, col // 2, col % 2
    y = 2 * yhi + ylo
    s = 1 - 2 * core

    def dev(zz, yy, xx, cc):
        return {"dp": zz * 2 + yy % 2, "row": xx, "col": (yy // 2) * 2 + cc}

    sources = [dev(z, 2 * (x // 2) + j, y, x % 2) for j in range(2)]
    targets = [dev(z, x, 2 * yhi + core, c) for c in range(2)]
    loops = (x == y) & (core == x % 2)
    z_f, z_b = dev((z + s + NZ) % NZ, y, x, core), dev((z - s + NZ) % NZ, y, x, core)
    y_f, y_b = dev(z, (y + s + NY) % NY, x, core), dev(z, (y - s + NY) % NY, x, core)
    sib = dev(z, y, x, 1 - core)
    y_2 = dev(z, (y + 2) % NY, x, core)
    x_f, x_b = dev(z, y, (x + s + NX) % NX, core), dev(z, y, (x - s + NX) % NX, core)
    x_2 = dev(z, y, (x + 2) % NX, core)
    xf1, xb1, xf2 = (x - s + NX) % NX, (x + s + NX) % NX, (x + 2) % NX
    yf1, yb1, yf2 = (y - s + NY) % NY, (y + s + NY) % NY, (y + 2) % NY

    sends, keys, sent = [], {}, [0]

    def rid(key):
        if key not in keys:
            keys[key] = len(keys)
        return rsem.at[keys[key]]

    def copy(src, dst, key, to):
        i = sent[0]
        sent[0] += 1
        return pltpu.make_async_remote_copy(src, dst, ssem.at[i], rid(key), device_id=to)

    def send(src, dst, key, to):
        c = copy(src, dst, key, to)
        c.start()
        sends.append(c)

    def arrived(dst, key):
        pltpu.make_async_remote_copy(dst, dst, ssem.at[0], rid(key), device_id=sib).wait_recv()

    in_c = pltpu.make_async_copy(inp, B0, lsem.at[18])
    scl_in = pltpu.make_async_copy(scl_hbm, scl, lsem.at[19])
    lev_in = pltpu.make_async_copy(lev, L, lsem.at[0])
    gh_in = pltpu.make_async_copy(gh, GH, lsem.at[1])
    in_c.start()
    scl_in.start()
    lev_in.start()
    gh_in.start()
    bar = pltpu.get_barrier_semaphore()
    partners = sources + targets + [x_f, x_b, x_2, z_f, z_b, y_f, y_b, y_2, sib]
    for d in partners:
        pl.semaphore_signal(bar, 1, device_id=d)
    in_c.wait()
    block = B0[...].astype(f32)
    for j in range(2):

        @pl.when(ylo == j)
        def _():
            SA[...] = block[8 * j:8 * j + U].astype(bf16)
            eight = block[U:] if j == 0 else block[:8]
            SB[...] = jnp.concatenate([eight[:, :BW], eight[:, BO:]], 0).astype(bf16)

    pl.semaphore_wait(bar, len(partners))

    r_mine = pl.ds(pl.multiple_of(core * 2 * U, U), U)
    r_other = pl.ds(pl.multiple_of((1 - core) * 2 * U, U), U)
    r_b = pl.ds(U, U)

    to_chip = dev(z, x, 2 * yhi + core, ylo)
    r_to = pl.ds(pl.multiple_of(ylo * 2 * U, U), U)
    swaps = []
    for src, dst, key in ((SA, X.at[x, 0, r_to], ("swap", 0)), (SB, RB.at[ylo], ("swap", 1))):
        swaps.append(pltpu.make_async_remote_copy(src, dst, ssem.at[sent[0]], rid(key), device_id=to_chip))
        sent[0] += 1

    @pl.when(jnp.logical_not(loops))
    def _():
        for c in swaps:
            c.start()

    @pl.when(loops)
    def _():
        X[y, 0, r_mine] = SA[...]
        RB[core] = SB[...]

    def weights(a0, a1):
        @pl.loop(a0, a1)
        def _(a):
            r = pl.ds(pl.multiple_of(a * 128, 128), 128)
            for b in range(H // 128):
                cs = pl.ds(b * 128, 128)
                W[r, cs] = (L[r, cs].astype(f32) * scl[b, a]).astype(bf16)

    def transposes(a0, a1):
        @pl.loop(a0, a1)
        def _(a):
            r = pl.ds(pl.multiple_of(a * 128, 128), 128)
            for b in range(H // 128):
                cs = pl.ds(b * 128, 128)
                WT[cs, r] = W[r, cs].astype(f32).T.astype(bf16)

    @pl.when(jnp.logical_not(loops))
    def _():
        arrived(X.at[y, 0, r_mine], ("swap", 0))

    def rest():
        send(X.at[y, 0, r_mine], X.at[y, 0, r_mine], ("hand", 0), sib)

        @pl.when(jnp.logical_not(loops))
        def _():
            arrived(RB.at[core], ("swap", 1))

        send(RB.at[core], RB.at[core], ("hand", 1), sib)
        scl_in.wait()
        lev_in.wait()
        weights(0, 3)
        arrived(RB.at[1 - core], ("hand", 1))
        eights = [RB[j].astype(f32) for j in range(2)]
        eights = [jnp.concatenate([v[:8], v[8:, BW - BO:]], 1) for v in eights]
        X[y, 0, U:2 * U] = jnp.concatenate(eights, 0).astype(bf16)

    c_mine = pl.ds(pl.multiple_of(core * BO, 128), BW)
    c_other = pl.ds(pl.multiple_of((1 - core) * BO, 128), BW)
    c_give = pl.ds(pl.multiple_of(core * BW, 128), BO)
    c_take = pl.ds(pl.multiple_of((1 - core) * BW, 128), BO)

    def a_unit(yq, p):
        return X.at[yq, p, r_mine]

    def b_unit(yq, p):
        return X.at[yq, p, r_b, c_mine]

    name_of = {id(y): "0", id(yf1): "f1", id(yb1): "b1", id(yf2): "f2"}

    def at_dist(k):
        return [0] if k == 0 else [pos_f(k)] + ([pos_b(k)] if k < 4 else [])

    def y_start(p):
        send(a_unit(y, p), a_unit(y, p), ("Ay", p, 1), y_f)
        send(a_unit(y, p), a_unit(y, p), ("Ay", p, -1), y_b)
        if p == 7:
            send(a_unit(y, p), a_unit(y, p), ("Ay", p, 2), y_2)

    def y_hop1(p):
        arrived(a_unit(yf1, p), ("Ay", p, 1))
        if p != 7:
            send(a_unit(yf1, p), a_unit(yf1, p), ("Ay", p, 2), y_f)
        if p == 0:
            send(a_unit(yf1, 0), a_unit(yf1, 0), ("As0", -1), sib)
        arrived(a_unit(yb1, p), ("Ay", p, -1))
        if p == 0:
            send(a_unit(yb1, 0), a_unit(yb1, 0), ("As0", 1), sib)

    def y_hop2(p):
        arrived(a_unit(yf2, p), ("Ay", p, 2))
        if p == 0:
            send(a_unit(yf2, 0), a_unit(yf2, 0), ("As0", 2), sib)
        else:
            send(X.at[:, p, r_mine], X.at[:, sib_pos(p), r_mine], ("As", sib_pos(p)), sib)

    def bz_send(yq, k):
        if k < 4:
            send(b_unit(yq, pos_f(k)), b_unit(yq, pos_f(k + 1)), ("Bz", name_of[id(yq)], pos_f(k + 1)), z_f)
        if k < 3:
            send(b_unit(yq, pos_b(k)), b_unit(yq, pos_b(k + 1)), ("Bz", name_of[id(yq)], pos_b(k + 1)), z_b)

    def bz_hop(yq, k):
        for p in at_dist(k):
            arrived(b_unit(yq, p), ("Bz", name_of[id(yq)], p))
        bz_send(yq, k)

    def b_give(k):
        for p in at_dist(k):
            send(X.at[:, p, r_b, c_give], X.at[:, sib_pos(p), r_b, c_give], ("Bs", sib_pos(p)), sib)

    def sib_wait(k):
        for p in at_dist(k):
            if p == 0:
                arrived(X.at[y, 0, r_other], ("hand", 0))
                for q, yq in ((1, yf1), (-1, yb1), (2, yf2)):
                    arrived(X.at[yq, 0, r_other], ("As0", q))
                    arrived(X.at[yq, 0, r_b, c_take], ("Bs0", q))
            else:
                arrived(X.at[:, p, r_other], ("As", p))
                arrived(X.at[:, p, r_b, c_take], ("Bs", p))

    def az_send(k):
        if k < 4:
            send(a_unit(y, pos_f(k)), a_unit(y, pos_f(k + 1)), ("Az", pos_f(k + 1)), z_f)
        if k < 3:
            send(a_unit(y, pos_b(k)), a_unit(y, pos_b(k + 1)), ("Az", pos_b(k + 1)), z_b)

    def tick(k):
        if k == 0:
            az_send(0)
            y_start(0)
            rest()
            for q, to in ((1, y_f), (-1, y_b), (2, y_2)):
                send(b_unit(y, 0), b_unit(y, 0), ("By", q), to)
            bz_send(y, 0)
            return
        if k <= 4:
            for p in at_dist(k):
                arrived(a_unit(y, p), ("Az", p))
            az_send(k)
            for p in at_dist(k):
                y_start(p)
        if k == 1:
            for q, yq, r in ((1, yf1, -1), (-1, yb1, 1), (2, yf2, 2)):
                arrived(b_unit(yq, 0), ("By", q))
                bz_send(yq, 0)
                send(X.at[yq, 0, r_b, c_give], X.at[yq, 0, r_b, c_give], ("Bs0", r), sib)
        if k <= 4:
            bz_hop(y, k)
        for p in at_dist(k - 1):
            y_hop1(p)
        if 2 <= k <= 5:
            for yq in (yf1, yb1, yf2):
                bz_hop(yq, k - 1)
            b_give(k - 1)
        if k >= 2:
            for p in at_dist(k - 2):
                y_hop2(p)
        if k == 5:
            y_hop2(7)

    def partial_pre(g):
        p0, p1 = GROUPS[g]
        m = (p1 - p0) * ROWS
        for h in range(0, H, 256):
            rows = X[:, p0:p1].reshape(NY * m, D4)
            part = jnp.dot(rows, W[:, h:h + 256], preferred_element_type=f32)
            PS[:, p0:p1, :, h:h + 256] = part.astype(bf16).reshape(NY, p1 - p0, ROWS, 256)
        send(PS.at[xf2, p0:p1], PR.at[0, p0:p1], ("pre", g, 0), x_2 if g >= DIRECT else x_b)
        send(PS.at[xb1, p0:p1], PR.at[1, p0:p1], ("pre", g, 1), x_f)
        if g >= DIRECT:
            send(PS.at[xf1, p0:p1], PR.at[2, p0:p1], ("pre", g, 2), x_b)

    def pre_middle(g):
        p0, p1 = GROUPS[g]
        arrived(PR.at[0, p0:p1], ("pre", g, 0))
        PM[p0:p1] = (PS[xf1, p0:p1].astype(f32) + PR[0, p0:p1].astype(f32)).astype(bf16)
        send(PM.at[p0:p1], PR.at[2, p0:p1], ("pre", g, 2), x_b)

    def activate(g):
        p0, p1 = GROUPS[g]
        parts = (0, 1, 2) if g >= DIRECT else (1, 2)
        for d in parts:
            arrived(PR.at[d, p0:p1], ("pre", g, d))

        @pl.loop(p0, p1)
        def _(p):
            k = (p + 1) // 2
            zz = (z + (1 - 2 * (p % 2)) * k * s + NZ) % NZ
            pre = PS[x, p].astype(f32)
            for d in parts:
                pre += PR[d, p].astype(f32)
            activated, slope = gelu_pair(pre)
            HD[zz] = activated.astype(bf16)
            GP[x, p] = (GH[zz].astype(f32) * slope).astype(bf16)

        own = GP.at[x, p0:p1]
        send(own, own, ("gp", g, 1), x_f)
        send(own, own, ("gp", g, -1), x_b)
        if g >= DIRECT:
            send(own, own, ("gp", g, 2), x_2)

    def grad_middle(g):
        p0, p1 = GROUPS[g]
        arrived(GP.at[xf1, p0:p1], ("gp", g, 1))
        send(GP.at[xf1, p0:p1], GP.at[xf1, p0:p1], ("gp", g, 2), x_f)

    def input_terms(g):
        p0, p1 = GROUPS[g]
        m = (p1 - p0) * ROWS
        if g >= DIRECT:
            arrived(GP.at[xf1, p0:p1], ("gp", g, 1))
        arrived(GP.at[xb1, p0:p1], ("gp", g, -1))
        arrived(GP.at[xf2, p0:p1], ("gp", g, 2))

        @pl.loop(0, D4 // 384)
        def _(n):
            cs = pl.ds(pl.multiple_of(n * 384, 128), 384)
            rows = GP[:, p0:p1].reshape(NY * m, H)
            part = jnp.dot(rows, WT[:, cs], preferred_element_type=f32)
            GI[:, p0:p1, :, cs] = part.astype(bf16).reshape(NY, p1 - p0, ROWS, 384)

        for p in reversed(range(p0, p1)):
            q = sib_pos(p)
            send(GI.at[:, p, r_b, c_other], CB.at[:, q], ("CB", q), sib)
            send(GI.at[:, p, r_other], CA.at[:, q], ("CA", q), sib)

    def a_term(yq, p):
        return GI[yq, p, r_mine].astype(f32) + CA[yq, p].astype(f32)

    def ay_begin(p):
        arrived(CA.at[:, p], ("CA", p))
        A1s[p] = a_term(yf2, p).astype(bf16)
        send(A1s.at[p], A1r.at[p], ("A1", p), y_2 if p >= 5 else y_b)
        if p >= 5:
            A2s[p] = a_term(yf1, p).astype(bf16)
            send(A2s.at[p], A2r.at[p], ("A2", p), y_b)
        Ass[p] = a_term(yb1, p).astype(bf16)
        send(Ass.at[p], Asr.at[p], ("As_", p), y_f)

    def ay_middle(p):
        arrived(A1r.at[p], ("A1", p))
        A2s[p] = (a_term(yf1, p) + A1r[p].astype(f32)).astype(bf16)
        send(A2s.at[p], A2r.at[p], ("A2", p), y_b)

    def ay_end(p):
        arrived(Asr.at[p], ("As_", p))
        arrived(A2r.at[p], ("A2", p))
        total = a_term(y, p) + Asr[p].astype(f32) + A2r[p].astype(f32)
        if p >= 5:
            arrived(A1r.at[p], ("A1", p))
            total += A1r[p].astype(f32)
        YA[p] = total

    def z_chain(j, term, at, ls, lr, ss, sr, name):
        if j == 0:
            at(ls, 0)[...] = term(pos_f(4)).astype(bf16)
        else:
            arrived(at(lr, j - 1), (name, "L", j))
            if j < 4:
                at(ls, j)[...] = (term(pos_f(4 - j)) + at(lr, j - 1)[...].astype(f32)).astype(bf16)
        if j < 4:
            send(at(ls, j), at(lr, j), (name, "L", j + 1), z_b)
        if j == 0:
            at(ss, 0)[...] = term(pos_b(3)).astype(bf16)
        elif j < 4:
            arrived(at(sr, j - 1), (name, "S", j))
            if j < 3:
                at(ss, j)[...] = (term(pos_b(3 - j)) + at(sr, j - 1)[...].astype(f32)).astype(bf16)
        if j < 3:
            send(at(ss, j), at(sr, j), (name, "S", j + 1), z_f)
        if j == 4:
            return term(0) + at(lr, 3)[...].astype(f32) + at(sr, 2)[...].astype(f32)

    outs = []

    def start_out(c):
        c.start()
        outs.append(c)

    def hidden_out():
        start_out(pltpu.make_async_copy(HD, hid, lsem.at[2]))

    def weight_tile(n, p0, p1):
        cs = pl.ds(pl.multiple_of(n * 128, 128), 128)
        rows = X[:, p0:p1, :, cs].reshape(NY * (p1 - p0) * ROWS, 128)
        grads = GP[:, p0:p1].reshape(NY * (p1 - p0) * ROWS, H)
        return cs, lax.dot_general(rows, grads, (((0,), (0,)), ((), ())), preferred_element_type=f32)

    def weight_far(n0, n1):
        @pl.loop(n0, n1)
        def _(n):
            cs, part = weight_tile(n, NEAR, NZ)
            GA[cs, :] = part

    def weight_grad(n0, n1):
        @pl.loop(n0, n1)
        def _(n):
            cs, part = weight_tile(n, 0, NEAR)
            GW[cs, :] = (GA[cs, :] + part).astype(bf16)

        r = pl.ds(n0 * 128, (n1 - n0) * 128)
        start_out(pltpu.make_async_copy(GW.at[r], gw.at[r], lsem.at[3 + n0]))

    def b_step(j, *rows):
        for yq in rows:
            nm = name_of[id(yq)]
            last = z_chain(
                j,
                lambda p: GI[yq, p, r_b, c_mine].astype(f32) + CB[yq, p].astype(f32),
                lambda buf, i: buf.at[i, yq],
                BLs, BLr, BSs, BSr, "B" + nm,
            )
            if j < 4:
                continue
            YB[yq] = last
            if nm == "f2":
                Y1s[...] = last.astype(bf16)
                send(Y1s, Y1r, ("Y1",), y_2)
            elif nm == "f1":
                Y2s[...] = last.astype(bf16)
                send(Y2s, Y2r, ("Y2",), y_b)
            elif nm == "b1":
                Yss[...] = last.astype(bf16)
                send(Yss, Ysr, ("Ys",), y_f)

    def b_end():
        arrived(Ysr, ("Ys",))
        arrived(Y2r, ("Y2",))
        arrived(Y1r, ("Y1",))
        FB[...] = (YB[y] + Ysr[...].astype(f32) + Y2r[...].astype(f32) + Y1r[...].astype(f32)).astype(bf16)

    def cb_wait(*ps):
        for p in ps:
            arrived(CB.at[:, p], ("CB", p))

    def a_step(j):
        last = z_chain(j, lambda p: YA[p], lambda buf, i: buf.at[i], ZLs, ZLr, ZSs, ZSr, "A")
        if j == 4:
            FA[...] = last.astype(bf16)

    backs = []
    rid(("OB", 0))
    rid(("OB", 1))
    b_sems = keys[("OB", 0)]

    def give_back(src, dst, sem, only):
        for j in range(2):
            other = jnp.logical_not(loops & (j == x % 2))
            which = other & (core == j) if only else other
            i = sent[0]
            sent[0] += 1
            c = pltpu.make_async_remote_copy(src, dst, ssem.at[i], sem, device_id=sources[j])
            backs.append((which, c))

            @pl.when(which)
            def _():
                c.start()

        @pl.when(loops)
        def _():
            dst[...] = src[...]

    def give_a():
        give_back(FA, OA, rid(("OA",)), True)

    def give_b():
        give_back(FB, OB.at[core], rsem.at[b_sems + core], False)

    def take_back():
        @pl.when(jnp.logical_not(loops))
        def _():
            arrived(OA, ("OA",))

        for c in range(2):

            @pl.when(jnp.logical_not(loops & (core == c)))
            def _():
                arrived(OB.at[c], ("OB", c))

        a_rows = OA[...].astype(f32)
        b_rows = jnp.concatenate([OB[0].astype(f32), OB[1].astype(f32)[:, 2 * BW - D4:]], 1)

        @pl.when(ylo == 0)
        def _():
            gin[...] = jnp.concatenate([a_rows, b_rows[:8]], 0).astype(bf16)

        @pl.when(ylo == 1)
        def _():
            gin[...] = jnp.concatenate([b_rows[8:], a_rows], 0).astype(bf16)

    steps = [
        (tick, 0), (weights, 3, 6), (gh_in.wait,),
        (tick, 1), (weights, 6, 11),
        (tick, 2), (weights, 11, 15),
        (sib_wait, 0), (partial_pre, 0),
        (tick, 3), (pre_middle, 0), (sib_wait, 1), (partial_pre, 1),
        (tick, 4), (activate, 0), (sib_wait, 2), (partial_pre, 2),
        (tick, 5), (pre_middle, 1), (grad_middle, 0),
        (sib_wait, 3), (partial_pre, 3), (pre_middle, 2), (sib_wait, 4), (partial_pre, 4),
        (transposes, 0, 15), (pre_middle, 3), (activate, 2), (activate, 4),
        (input_terms, 0), (activate, 3), (activate, 1), (hidden_out,),
        (grad_middle, 2), (ay_begin, 0),
        (input_terms, 4), (ay_middle, 0), (grad_middle, 3),
        (input_terms, 2), (ay_begin, 7), (ay_begin, 3), (ay_begin, 4), (grad_middle, 1),
        (input_terms, 3),
        (ay_end, 0), (cb_wait, 7, 6, 5),
        (b_step, 0, yf2, yf1, yb1, y),
        (ay_begin, 6), (ay_begin, 5), (ay_end, 7), (ay_middle, 3), (ay_middle, 4),
        (input_terms, 1),
        (cb_wait, 4, 3),
        (b_step, 1, yf2, yf1, yb1, y),
        (ay_end, 6), (a_step, 0), (ay_end, 5),
        (cb_wait, 2, 1, 0), (ay_begin, 2), (ay_begin, 1), (ay_end, 4), (ay_end, 3),
        (b_step, 2, yf2, yf1, yb1, y),
        (a_step, 1),
        (weight_far, 0, 3),
        (ay_middle, 2), (ay_middle, 1),
        (b_step, 3, yf2, yf1, yb1, y),
        (weight_far, 3, 5),
        (ay_end, 2), (a_step, 2), (ay_end, 1),
        (b_step, 4, yf2, yf1, yb1, y),
        (weight_far, 5, 9),
        (a_step, 3),
        (weight_far, 9, 15),
        (b_end,), (give_b,),
        (a_step, 4), (give_a,),
        (weight_grad, 0, 15),
        (take_back,),
    ]
    for step, *args in steps:
        step(*args)

    @pl.when(jnp.logical_not(loops))
    def _():
        for c in swaps:
            c.wait_send()

    for which, c in backs:

        @pl.when(which)
        def _():
            c.wait_send()

    for c in sends:
        c.wait_send()
    for c in outs:
        c.wait()
    assert sent[0] <= N_SEND and len(keys) <= N_RECV, (sent, len(keys))


def flush(h, i, w, ho, io, wo, sem):
    cut = [pl.ds(n * (D4 // 4), D4 // 4) for n in range(4)]
    parts = [(w.at[r], wo.at[r]) for r in cut] + [(h, ho), (i, io)]
    copies = [pltpu.make_async_copy(a, o, sem.at[n]) for n, (a, o) in enumerate(parts)]
    for c in copies:
        c.start()
    for c in copies:
        c.wait()


def shards(inputs, levels, block_scales, grad_hidden):
    vm = lambda *shape: pltpu.VMEM(shape, bf16)
    vf = lambda *shape: pltpu.VMEM(shape, f32)
    vmem = pl.BlockSpec(memory_space=pltpu.VMEM)
    hbm, far = pl.BlockSpec(memory_space=pl.ANY), pl.BlockSpec(memory_space=pltpu.HBM)
    stay = lambda a: pltpu.with_memory_space_constraint(a, pltpu.HBM)
    a_buf = vm(NZ, U, D4)
    y_buf = vm(U, BW)
    out_shape = (
        jax.ShapeDtypeStruct((NZ, ROWS, H), bf16),
        jax.ShapeDtypeStruct((24, D4), bf16),
        jax.ShapeDtypeStruct((D4, H), bf16),
    )
    outs = pl.pallas_call(
        kernel,
        out_shape=out_shape,
        in_specs=[far, far, far, far],
        out_specs=(hbm, vmem, hbm),
        scratch_shapes=[
            vm(24, D4), pltpu.SMEM((H // 128, D4 // 128), f32),
            vm(D4, H), vm(D4, H), vm(H, D4),
            vm(U, D4), y_buf, vm(2, U, BW),
            vm(NY, NZ, ROWS, D4),
            vm(NZ, ROWS, H), vm(NZ, ROWS, H),
            vm(NY, NZ, ROWS, H), vm(NX - 1, NZ, ROWS, H), vm(NZ, ROWS, H), vm(NY, NZ, ROWS, H),
            vm(NY, NZ, ROWS, D4), vf(D4, H), vm(D4, H),
            vm(NY, NZ, U, D4), vm(NY, NZ, U, BW),
            a_buf, a_buf, a_buf, a_buf, a_buf, a_buf, vf(NZ, U, D4),
            vm(4, U, D4), vm(4, U, D4), vm(3, U, D4), vm(3, U, D4),
            vm(4, NY, U, BW), vm(4, NY, U, BW), vm(3, NY, U, BW), vm(3, NY, U, BW), vf(NY, U, BW),
            y_buf, y_buf, y_buf, y_buf, y_buf, y_buf,
            vm(U, D4), y_buf, vm(U, D4), vm(2, U, BW),
            pltpu.SemaphoreType.DMA((N_SEND,)),
            pltpu.SemaphoreType.DMA((N_RECV,)),
            pltpu.SemaphoreType.DMA((24,)),
        ],
        compiler_params=pltpu.CompilerParams(
            collective_id=0, has_side_effects=True, vmem_limit_bytes=46 * 2**20
        ),
        name="grid_layer",
    )(stay(inputs[0]), stay(levels), stay(block_scales.T), stay(grad_hidden.reshape(NZ, ROWS, H)))
    hidden, grad_inputs, grad_weight = pl.pallas_call(
        flush,
        out_shape=out_shape,
        in_specs=[hbm] * 3,
        out_specs=(hbm,) * 3,
        scratch_shapes=[pltpu.SemaphoreType.DMA((6,))],
        compiler_params=pltpu.CompilerParams(vmem_limit_bytes=2**20),
        name="flush",
    )(*outs)
    return (hidden.reshape(grad_hidden.shape), grad_inputs[None], grad_weight)


def solution(mesh):
    placed = (
        P("dp", "row", "col"),
        P("row", ("dp", "col")),
        P("row", ("dp", "col")),
        P(None, "row", ("dp", "col")),
    )
    return jax.shard_map(
        shards,
        mesh=mesh,
        in_specs=placed,
        out_specs=(P(None, "row", ("dp", "col")), P("dp", "row", "col"), P("row", ("dp", "col"))),
        check_vma=False,
    )
```

```python
import jax
import jax.numpy as jnp
from jax import lax
from jax.experimental import pallas as pl
from jax.experimental.pallas import tpu as pltpu
from jax.sharding import PartitionSpec as P

inv_root_two = 0.7071067811865476
inv_root_two_pi = 0.3989422804014327
bf16, f32 = jnp.bfloat16, jnp.float32

NZ, NY, NX = 8, 4, 4
ROWS = 48
U = 16
D4 = 1920
H = 512
BW = 1024
BO = 896
GROUPS = ((0, 1), (1, 3), (3, 5), (5, 7), (7, 8))
NEAR = 3
DIRECT = 4
N_SEND, N_RECV = 208, 208


def pos_f(k):
    return 0 if k == 0 else 2 * k - 1


def pos_b(k):
    return 2 * k


def sib_pos(p):
    if p == 0 or p == 7:
        return p
    return p + 1 if p % 2 else p - 1


def gelu_pair(pre):
    normal_cdf = 0.5 * (1.0 + lax.erf(pre * inv_root_two))
    density = jnp.exp(-0.5 * pre * pre) * inv_root_two_pi
    return (pre * normal_cdf, normal_cdf + pre * density)


def kernel(inp, lev, scl_hbm, gh, hid, gin, gw,
           B0, scl, L, W, WT, SA, SB, RB, X, GH, HD, PS, PR, PM, GP, GI, GA, GW, CA, CB,
           A1s, Ass, A2s, A1r, Asr, A2r, YA,
           ZLs, ZLr, ZSs, ZSr, BLs, BLr, BSs, BSr, YB,
           Y1s, Yss, Y2s, Y1r, Ysr, Y2r, FA, FB, OA, OB,
           ssem, rsem, lsem):
    dp, x, col = lax.axis_index("dp"), lax.axis_index("row"), lax.axis_index("col")
    z, ylo, yhi, core = dp // 2, dp % 2, col // 2, col % 2
    y = 2 * yhi + ylo
    s = 1 - 2 * core

    def dev(zz, yy, xx, cc):
        return {"dp": zz * 2 + yy % 2, "row": xx, "col": (yy // 2) * 2 + cc}

    sources = [dev(z, 2 * (x // 2) + j, y, x % 2) for j in range(2)]
    targets = [dev(z, x, 2 * yhi + core, c) for c in range(2)]
    loops = (x == y) & (core == x % 2)
    z_f, z_b = dev((z + s + NZ) % NZ, y, x, core), dev((z - s + NZ) % NZ, y, x, core)
    y_f, y_b = dev(z, (y + s + NY) % NY, x, core), dev(z, (y - s + NY) % NY, x, core)
    sib = dev(z, y, x, 1 - core)
    y_2 = dev(z, (y + 2) % NY, x, core)
    x_f, x_b = dev(z, y, (x + s + NX) % NX, core), dev(z, y, (x - s + NX) % NX, core)
    x_2 = dev(z, y, (x + 2) % NX, core)
    xf1, xb1, xf2 = (x - s + NX) % NX, (x + s + NX) % NX, (x + 2) % NX
    yf1, yb1, yf2 = (y - s + NY) % NY, (y + s + NY) % NY, (y + 2) % NY

    sends, keys, sent = [], {}, [0]

    def rid(key):
        if key not in keys:
            keys[key] = len(keys)
        return rsem.at[keys[key]]

    def copy(src, dst, key, to):
        i = sent[0]
        sent[0] += 1
        return pltpu.make_async_remote_copy(src, dst, ssem.at[i], rid(key), device_id=to)

    def send(src, dst, key, to):
        c = copy(src, dst, key, to)
        c.start()
        sends.append(c)

    def arrived(dst, key):
        pltpu.make_async_remote_copy(dst, dst, ssem.at[0], rid(key), device_id=sib).wait_recv()

    in_c = pltpu.make_async_copy(inp, B0, lsem.at[18])
    scl_in = pltpu.make_async_copy(scl_hbm, scl, lsem.at[19])
    lev_in = pltpu.make_async_copy(lev, L, lsem.at[0])
    gh_in = pltpu.make_async_copy(gh, GH, lsem.at[1])
    in_c.start()
    scl_in.start()
    lev_in.start()
    gh_in.start()
    bar = pltpu.get_barrier_semaphore()
    partners = sources + targets + [x_f, x_b, x_2, z_f, z_b, y_f, y_b, y_2, sib]
    for d in partners:
        pl.semaphore_signal(bar, 1, device_id=d)
    in_c.wait()
    block = B0[...].astype(f32)
    for j in range(2):

        @pl.when(ylo == j)
        def _():
            SA[...] = block[8 * j:8 * j + U].astype(bf16)
            eight = block[U:] if j == 0 else block[:8]
            SB[...] = jnp.concatenate([eight[:, :BW], eight[:, BO:]], 0).astype(bf16)

    pl.semaphore_wait(bar, len(partners))

    r_mine = pl.ds(pl.multiple_of(core * 2 * U, U), U)
    r_other = pl.ds(pl.multiple_of((1 - core) * 2 * U, U), U)
    r_b = pl.ds(U, U)

    to_chip = dev(z, x, 2 * yhi + core, ylo)
    r_to = pl.ds(pl.multiple_of(ylo * 2 * U, U), U)
    swaps = []
    for src, dst, key in ((SA, X.at[x, 0, r_to], ("swap", 0)), (SB, RB.at[ylo], ("swap", 1))):
        swaps.append(pltpu.make_async_remote_copy(src, dst, ssem.at[sent[0]], rid(key), device_id=to_chip))
        sent[0] += 1

    @pl.when(jnp.logical_not(loops))
    def _():
        for c in swaps:
            c.start()

    @pl.when(loops)
    def _():
        X[y, 0, r_mine] = SA[...]
        RB[core] = SB[...]

    def weights(a0, a1):
        @pl.loop(a0, a1)
        def _(a):
            r = pl.ds(pl.multiple_of(a * 128, 128), 128)
            for b in range(H // 128):
                cs = pl.ds(b * 128, 128)
                W[r, cs] = (L[r, cs].astype(f32) * scl[b, a]).astype(bf16)

    def transposes(a0, a1):
        @pl.loop(a0, a1)
        def _(a):
            r = pl.ds(pl.multiple_of(a * 128, 128), 128)
            for b in range(H // 128):
                cs = pl.ds(b * 128, 128)
                WT[cs, r] = W[r, cs].astype(f32).T.astype(bf16)

    @pl.when(jnp.logical_not(loops))
    def _():
        arrived(X.at[y, 0, r_mine], ("swap", 0))

    def rest():
        send(X.at[y, 0, r_mine], X.at[y, 0, r_mine], ("hand", 0), sib)

        @pl.when(jnp.logical_not(loops))
        def _():
            arrived(RB.at[core], ("swap", 1))

        send(RB.at[core], RB.at[core], ("hand", 1), sib)
        scl_in.wait()
        lev_in.wait()
        weights(0, 3)
        arrived(RB.at[1 - core], ("hand", 1))
        eights = [RB[j].astype(f32) for j in range(2)]
        eights = [jnp.concatenate([v[:8], v[8:, BW - BO:]], 1) for v in eights]
        X[y, 0, U:2 * U] = jnp.concatenate(eights, 0).astype(bf16)

    c_mine = pl.ds(pl.multiple_of(core * BO, 128), BW)
    c_other = pl.ds(pl.multiple_of((1 - core) * BO, 128), BW)
    c_give = pl.ds(pl.multiple_of(core * BW, 128), BO)
    c_take = pl.ds(pl.multiple_of((1 - core) * BW, 128), BO)

    def a_unit(yq, p):
        return X.at[yq, p, r_mine]

    def b_unit(yq, p):
        return X.at[yq, p, r_b, c_mine]

    name_of = {id(y): "0", id(yf1): "f1", id(yb1): "b1", id(yf2): "f2"}

    def at_dist(k):
        return [0] if k == 0 else [pos_f(k)] + ([pos_b(k)] if k < 4 else [])

    def y_start(p):
        send(a_unit(y, p), a_unit(y, p), ("Ay", p, 1), y_f)
        send(a_unit(y, p), a_unit(y, p), ("Ay", p, -1), y_b)
        if p == 7:
            send(a_unit(y, p), a_unit(y, p), ("Ay", p, 2), y_2)

    def y_hop1(p):
        arrived(a_unit(yf1, p), ("Ay", p, 1))
        if p != 7:
            send(a_unit(yf1, p), a_unit(yf1, p), ("Ay", p, 2), y_f)
        if p == 0:
            send(a_unit(yf1, 0), a_unit(yf1, 0), ("As0", -1), sib)
        arrived(a_unit(yb1, p), ("Ay", p, -1))
        if p == 0:
            send(a_unit(yb1, 0), a_unit(yb1, 0), ("As0", 1), sib)

    def y_hop2(p):
        arrived(a_unit(yf2, p), ("Ay", p, 2))
        if p == 0:
            send(a_unit(yf2, 0), a_unit(yf2, 0), ("As0", 2), sib)
        else:
            send(X.at[:, p, r_mine], X.at[:, sib_pos(p), r_mine], ("As", sib_pos(p)), sib)

    def bz_send(yq, k):
        if k < 4:
            send(b_unit(yq, pos_f(k)), b_unit(yq, pos_f(k + 1)), ("Bz", name_of[id(yq)], pos_f(k + 1)), z_f)
        if k < 3:
            send(b_unit(yq, pos_b(k)), b_unit(yq, pos_b(k + 1)), ("Bz", name_of[id(yq)], pos_b(k + 1)), z_b)

    def bz_hop(yq, k):
        for p in at_dist(k):
            arrived(b_unit(yq, p), ("Bz", name_of[id(yq)], p))
        bz_send(yq, k)

    def b_give(k):
        for p in at_dist(k):
            send(X.at[:, p, r_b, c_give], X.at[:, sib_pos(p), r_b, c_give], ("Bs", sib_pos(p)), sib)

    def sib_wait(k):
        for p in at_dist(k):
            if p == 0:
                arrived(X.at[y, 0, r_other], ("hand", 0))
                for q, yq in ((1, yf1), (-1, yb1), (2, yf2)):
                    arrived(X.at[yq, 0, r_other], ("As0", q))
                    arrived(X.at[yq, 0, r_b, c_take], ("Bs0", q))
            else:
                arrived(X.at[:, p, r_other], ("As", p))
                arrived(X.at[:, p, r_b, c_take], ("Bs", p))

    def az_send(k):
        if k < 4:
            send(a_unit(y, pos_f(k)), a_unit(y, pos_f(k + 1)), ("Az", pos_f(k + 1)), z_f)
        if k < 3:
            send(a_unit(y, pos_b(k)), a_unit(y, pos_b(k + 1)), ("Az", pos_b(k + 1)), z_b)

    def tick(k):
        if k == 0:
            az_send(0)
            y_start(0)
            rest()
            for q, to in ((1, y_f), (-1, y_b), (2, y_2)):
                send(b_unit(y, 0), b_unit(y, 0), ("By", q), to)
            bz_send(y, 0)
            return
        if k <= 4:
            for p in at_dist(k):
                arrived(a_unit(y, p), ("Az", p))
            az_send(k)
            for p in at_dist(k):
                y_start(p)
        if k == 1:
            for q, yq, r in ((1, yf1, -1), (-1, yb1, 1), (2, yf2, 2)):
                arrived(b_unit(yq, 0), ("By", q))
                bz_send(yq, 0)
                send(X.at[yq, 0, r_b, c_give], X.at[yq, 0, r_b, c_give], ("Bs0", r), sib)
        if k <= 4:
            bz_hop(y, k)
        for p in at_dist(k - 1):
            y_hop1(p)
        if 2 <= k <= 5:
            for yq in (yf1, yb1, yf2):
                bz_hop(yq, k - 1)
            b_give(k - 1)
        if k >= 2:
            for p in at_dist(k - 2):
                y_hop2(p)
        if k == 5:
            y_hop2(7)

    def partial_pre(g):
        p0, p1 = GROUPS[g]
        m = (p1 - p0) * ROWS
        for h in range(0, H, 256):
            rows = X[:, p0:p1].reshape(NY * m, D4)
            part = jnp.dot(rows, W[:, h:h + 256], preferred_element_type=f32)
            PS[:, p0:p1, :, h:h + 256] = part.astype(bf16).reshape(NY, p1 - p0, ROWS, 256)
        send(PS.at[xf2, p0:p1], PR.at[0, p0:p1], ("pre", g, 0), x_2 if g >= DIRECT else x_b)
        send(PS.at[xb1, p0:p1], PR.at[1, p0:p1], ("pre", g, 1), x_f)
        if g >= DIRECT:
            send(PS.at[xf1, p0:p1], PR.at[2, p0:p1], ("pre", g, 2), x_b)

    def pre_middle(g):
        p0, p1 = GROUPS[g]
        arrived(PR.at[0, p0:p1], ("pre", g, 0))
        PM[p0:p1] = (PS[xf1, p0:p1].astype(f32) + PR[0, p0:p1].astype(f32)).astype(bf16)
        send(PM.at[p0:p1], PR.at[2, p0:p1], ("pre", g, 2), x_b)

    def activate(g):
        p0, p1 = GROUPS[g]
        parts = (0, 1, 2) if g >= DIRECT else (1, 2)
        for d in parts:
            arrived(PR.at[d, p0:p1], ("pre", g, d))

        @pl.loop(p0, p1)
        def _(p):
            k = (p + 1) // 2
            zz = (z + (1 - 2 * (p % 2)) * k * s + NZ) % NZ
            pre = PS[x, p].astype(f32)
            for d in parts:
                pre += PR[d, p].astype(f32)
            activated, slope = gelu_pair(pre)
            HD[zz] = activated.astype(bf16)
            GP[x, p] = (GH[zz].astype(f32) * slope).astype(bf16)

        own = GP.at[x, p0:p1]
        send(own, own, ("gp", g, 1), x_f)
        send(own, own, ("gp", g, -1), x_b)
        if g >= DIRECT:
            send(own, own, ("gp", g, 2), x_2)

    def grad_middle(g):
        p0, p1 = GROUPS[g]
        arrived(GP.at[xf1, p0:p1], ("gp", g, 1))
        send(GP.at[xf1, p0:p1], GP.at[xf1, p0:p1], ("gp", g, 2), x_f)

    def input_terms(g):
        p0, p1 = GROUPS[g]
        m = (p1 - p0) * ROWS
        if g >= DIRECT:
            arrived(GP.at[xf1, p0:p1], ("gp", g, 1))
        arrived(GP.at[xb1, p0:p1], ("gp", g, -1))
        arrived(GP.at[xf2, p0:p1], ("gp", g, 2))

        @pl.loop(0, D4 // 384)
        def _(n):
            cs = pl.ds(pl.multiple_of(n * 384, 128), 384)
            rows = GP[:, p0:p1].reshape(NY * m, H)
            part = jnp.dot(rows, WT[:, cs], preferred_element_type=f32)
            GI[:, p0:p1, :, cs] = part.astype(bf16).reshape(NY, p1 - p0, ROWS, 384)

        for p in reversed(range(p0, p1)):
            q = sib_pos(p)
            send(GI.at[:, p, r_b, c_other], CB.at[:, q], ("CB", q), sib)
            send(GI.at[:, p, r_other], CA.at[:, q], ("CA", q), sib)

    def a_term(yq, p):
        return GI[yq, p, r_mine].astype(f32) + CA[yq, p].astype(f32)

    def ay_begin(p):
        arrived(CA.at[:, p], ("CA", p))
        A1s[p] = a_term(yf2, p).astype(bf16)
        send(A1s.at[p], A1r.at[p], ("A1", p), y_2 if p >= 5 else y_b)
        if p >= 5:
            A2s[p] = a_term(yf1, p).astype(bf16)
            send(A2s.at[p], A2r.at[p], ("A2", p), y_b)
        Ass[p] = a_term(yb1, p).astype(bf16)
        send(Ass.at[p], Asr.at[p], ("As_", p), y_f)

    def ay_middle(p):
        arrived(A1r.at[p], ("A1", p))
        A2s[p] = (a_term(yf1, p) + A1r[p].astype(f32)).astype(bf16)
        send(A2s.at[p], A2r.at[p], ("A2", p), y_b)

    def ay_end(p):
        arrived(Asr.at[p], ("As_", p))
        arrived(A2r.at[p], ("A2", p))
        total = a_term(y, p) + Asr[p].astype(f32) + A2r[p].astype(f32)
        if p >= 5:
            arrived(A1r.at[p], ("A1", p))
            total += A1r[p].astype(f32)
        YA[p] = total

    def z_chain(j, term, at, ls, lr, ss, sr, name):
        if j == 0:
            at(ls, 0)[...] = term(pos_f(4)).astype(bf16)
        else:
            arrived(at(lr, j - 1), (name, "L", j))
            if j < 4:
                at(ls, j)[...] = (term(pos_f(4 - j)) + at(lr, j - 1)[...].astype(f32)).astype(bf16)
        if j < 4:
            send(at(ls, j), at(lr, j), (name, "L", j + 1), z_b)
        if j == 0:
            at(ss, 0)[...] = term(pos_b(3)).astype(bf16)
        elif j < 4:
            arrived(at(sr, j - 1), (name, "S", j))
            if j < 3:
                at(ss, j)[...] = (term(pos_b(3 - j)) + at(sr, j - 1)[...].astype(f32)).astype(bf16)
        if j < 3:
            send(at(ss, j), at(sr, j), (name, "S", j + 1), z_f)
        if j == 4:
            return term(0) + at(lr, 3)[...].astype(f32) + at(sr, 2)[...].astype(f32)

    outs = []

    def start_out(c):
        c.start()
        outs.append(c)

    def hidden_out():
        start_out(pltpu.make_async_copy(HD, hid, lsem.at[2]))

    def weight_tile(n, p0, p1):
        cs = pl.ds(pl.multiple_of(n * 128, 128), 128)
        rows = X[:, p0:p1, :, cs].reshape(NY * (p1 - p0) * ROWS, 128)
        grads = GP[:, p0:p1].reshape(NY * (p1 - p0) * ROWS, H)
        return cs, lax.dot_general(rows, grads, (((0,), (0,)), ((), ())), preferred_element_type=f32)

    def weight_far(n0, n1):
        @pl.loop(n0, n1)
        def _(n):
            cs, part = weight_tile(n, NEAR, NZ)
            GA[cs, :] = part

    def weight_grad(n0, n1):
        @pl.loop(n0, n1)
        def _(n):
            cs, part = weight_tile(n, 0, NEAR)
            GW[cs, :] = (GA[cs, :] + part).astype(bf16)

        r = pl.ds(n0 * 128, (n1 - n0) * 128)
        start_out(pltpu.make_async_copy(GW.at[r], gw.at[r], lsem.at[3 + n0]))

    def b_step(j, *rows):
        for yq in rows:
            nm = name_of[id(yq)]
            last = z_chain(
                j,
                lambda p: GI[yq, p, r_b, c_mine].astype(f32) + CB[yq, p].astype(f32),
                lambda buf, i: buf.at[i, yq],
                BLs, BLr, BSs, BSr, "B" + nm,
            )
            if j < 4:
                continue
            YB[yq] = last
            if nm == "f2":
                Y1s[...] = last.astype(bf16)
                send(Y1s, Y1r, ("Y1",), y_2)
            elif nm == "f1":
                Y2s[...] = last.astype(bf16)
                send(Y2s, Y2r, ("Y2",), y_b)
            elif nm == "b1":
                Yss[...] = last.astype(bf16)
                send(Yss, Ysr, ("Ys",), y_f)

    def b_end():
        arrived(Ysr, ("Ys",))
        arrived(Y2r, ("Y2",))
        arrived(Y1r, ("Y1",))
        FB[...] = (YB[y] + Ysr[...].astype(f32) + Y2r[...].astype(f32) + Y1r[...].astype(f32)).astype(bf16)

    def cb_wait(*ps):
        for p in ps:
            arrived(CB.at[:, p], ("CB", p))

    def a_step(j):
        last = z_chain(j, lambda p: YA[p], lambda buf, i: buf.at[i], ZLs, ZLr, ZSs, ZSr, "A")
        if j == 4:
            FA[...] = last.astype(bf16)

    backs = []
    rid(("OB", 0))
    rid(("OB", 1))
    b_sems = keys[("OB", 0)]

    def give_back(src, dst, sem, only):
        for j in range(2):
            other = jnp.logical_not(loops & (j == x % 2))
            which = other & (core == j) if only else other
            i = sent[0]
            sent[0] += 1
            c = pltpu.make_async_remote_copy(src, dst, ssem.at[i], sem, device_id=sources[j])
            backs.append((which, c))

            @pl.when(which)
            def _():
                c.start()

        @pl.when(loops)
        def _():
            dst[...] = src[...]

    def give_a():
        give_back(FA, OA, rid(("OA",)), True)

    def give_b():
        give_back(FB, OB.at[core], rsem.at[b_sems + core], False)

    def take_back():
        @pl.when(jnp.logical_not(loops))
        def _():
            arrived(OA, ("OA",))

        for c in range(2):

            @pl.when(jnp.logical_not(loops & (core == c)))
            def _():
                arrived(OB.at[c], ("OB", c))

        a_rows = OA[...].astype(f32)
        b_rows = jnp.concatenate([OB[0].astype(f32), OB[1].astype(f32)[:, 2 * BW - D4:]], 1)

        @pl.when(ylo == 0)
        def _():
            gin[...] = jnp.concatenate([a_rows, b_rows[:8]], 0).astype(bf16)

        @pl.when(ylo == 1)
        def _():
            gin[...] = jnp.concatenate([b_rows[8:], a_rows], 0).astype(bf16)

    steps = [
        (tick, 0), (weights, 3, 6), (gh_in.wait,),
        (tick, 1), (weights, 6, 11),
        (tick, 2), (weights, 11, 15),
        (sib_wait, 0), (partial_pre, 0),
        (tick, 3), (pre_middle, 0), (sib_wait, 1), (partial_pre, 1),
        (tick, 4), (activate, 0), (sib_wait, 2), (partial_pre, 2),
        (tick, 5), (pre_middle, 1), (grad_middle, 0),
        (sib_wait, 3), (partial_pre, 3), (pre_middle, 2), (sib_wait, 4), (partial_pre, 4),
        (transposes, 0, 15), (pre_middle, 3), (activate, 2), (activate, 4),
        (input_terms, 0), (activate, 3), (activate, 1), (hidden_out,),
        (grad_middle, 2), (ay_begin, 0),
        (input_terms, 4), (ay_middle, 0), (grad_middle, 3),
        (input_terms, 2), (ay_begin, 7), (ay_begin, 3), (ay_begin, 4), (grad_middle, 1),
        (input_terms, 3),
        (ay_end, 0), (cb_wait, 7, 6, 5),
        (b_step, 0, yf2, yf1, yb1, y),
        (ay_begin, 6), (ay_begin, 5), (ay_end, 7), (ay_middle, 3), (ay_middle, 4),
        (input_terms, 1),
        (cb_wait, 4, 3),
        (b_step, 1, yf2, yf1, yb1, y),
        (ay_end, 6), (a_step, 0), (ay_end, 5),
        (cb_wait, 2, 1, 0), (ay_begin, 2), (ay_begin, 1), (ay_end, 4), (ay_end, 3),
        (b_step, 2, yf2, yf1, yb1, y),
        (a_step, 1),
        (weight_far, 0, 3),
        (ay_middle, 2), (ay_middle, 1),
        (b_step, 3, yf2, yf1, yb1, y),
        (weight_far, 3, 5),
        (ay_end, 2), (a_step, 2), (ay_end, 1),
        (b_step, 4, yf2, yf1, yb1, y),
        (weight_far, 5, 9),
        (a_step, 3),
        (weight_far, 9, 15),
        (b_end,), (give_b,),
        (a_step, 4), (give_a,),
        (weight_grad, 0, 5), (weight_grad, 5, 9), (weight_grad, 9, 12), (weight_grad, 12, 15),
        (take_back,),
    ]
    for step, *args in steps:
        step(*args)

    @pl.when(jnp.logical_not(loops))
    def _():
        for c in swaps:
            c.wait_send()

    for which, c in backs:

        @pl.when(which)
        def _():
            c.wait_send()

    for c in sends:
        c.wait_send()
    for c in outs:
        c.wait()
    assert sent[0] <= N_SEND and len(keys) <= N_RECV, (sent, len(keys))


def flush(h, i, w, ho, io, wo, sem):
    cut = [pl.ds(n * (D4 // 4), D4 // 4) for n in range(4)]
    parts = [(w.at[r], wo.at[r]) for r in cut] + [(h, ho), (i, io)]
    copies = [pltpu.make_async_copy(a, o, sem.at[n]) for n, (a, o) in enumerate(parts)]
    for c in copies:
        c.start()
    for c in copies:
        c.wait()


def shards(inputs, levels, block_scales, grad_hidden):
    vm = lambda *shape: pltpu.VMEM(shape, bf16)
    vf = lambda *shape: pltpu.VMEM(shape, f32)
    vmem = pl.BlockSpec(memory_space=pltpu.VMEM)
    hbm, far = pl.BlockSpec(memory_space=pl.ANY), pl.BlockSpec(memory_space=pltpu.HBM)
    stay = lambda a: pltpu.with_memory_space_constraint(a, pltpu.HBM)
    a_buf = vm(NZ, U, D4)
    y_buf = vm(U, BW)
    out_shape = (
        jax.ShapeDtypeStruct((NZ, ROWS, H), bf16),
        jax.ShapeDtypeStruct((24, D4), bf16),
        jax.ShapeDtypeStruct((D4, H), bf16),
    )
    outs = pl.pallas_call(
        kernel,
        out_shape=out_shape,
        in_specs=[far, far, far, far],
        out_specs=(hbm, vmem, hbm),
        scratch_shapes=[
            vm(24, D4), pltpu.SMEM((H // 128, D4 // 128), f32),
            vm(D4, H), vm(D4, H), vm(H, D4),
            vm(U, D4), y_buf, vm(2, U, BW),
            vm(NY, NZ, ROWS, D4),
            vm(NZ, ROWS, H), vm(NZ, ROWS, H),
            vm(NY, NZ, ROWS, H), vm(NX - 1, NZ, ROWS, H), vm(NZ, ROWS, H), vm(NY, NZ, ROWS, H),
            vm(NY, NZ, ROWS, D4), vf(D4, H), vm(D4, H),
            vm(NY, NZ, U, D4), vm(NY, NZ, U, BW),
            a_buf, a_buf, a_buf, a_buf, a_buf, a_buf, vf(NZ, U, D4),
            vm(4, U, D4), vm(4, U, D4), vm(3, U, D4), vm(3, U, D4),
            vm(4, NY, U, BW), vm(4, NY, U, BW), vm(3, NY, U, BW), vm(3, NY, U, BW), vf(NY, U, BW),
            y_buf, y_buf, y_buf, y_buf, y_buf, y_buf,
            vm(U, D4), y_buf, vm(U, D4), vm(2, U, BW),
            pltpu.SemaphoreType.DMA((N_SEND,)),
            pltpu.SemaphoreType.DMA((N_RECV,)),
            pltpu.SemaphoreType.DMA((24,)),
        ],
        compiler_params=pltpu.CompilerParams(
            collective_id=0, has_side_effects=True, vmem_limit_bytes=46 * 2**20
        ),
        name="grid_layer",
    )(stay(inputs[0]), stay(levels), stay(block_scales.T), stay(grad_hidden.reshape(NZ, ROWS, H)))
    hidden, grad_inputs, grad_weight = pl.pallas_call(
        flush,
        out_shape=out_shape,
        in_specs=[hbm] * 3,
        out_specs=(hbm,) * 3,
        scratch_shapes=[pltpu.SemaphoreType.DMA((6,))],
        compiler_params=pltpu.CompilerParams(vmem_limit_bytes=2**20),
        name="flush",
    )(*outs)
    return (hidden.reshape(grad_hidden.shape), grad_inputs[None], grad_weight)


def solution(mesh):
    placed = (
        P("dp", "row", "col"),
        P("row", ("dp", "col")),
        P("row", ("dp", "col")),
        P(None, "row", ("dp", "col")),
    )
    return jax.shard_map(
        shards,
        mesh=mesh,
        in_specs=placed,
        out_specs=(P(None, "row", ("dp", "col")), P("dp", "row", "col"), P("row", ("dp", "col"))),
        check_vma=False,
    )
```
